128 devices in a mesh: layer: 32 (over z, y, x_lo), row: 2 (over core), col: 2 (over x_hi).
Axes of the slice: x: 4 (x_hi: 2, x_lo: 2; x = x_hi * 2 + x_lo), y: 4, z: 4, core: 2. Of those that a mesh axis runs over, the one named last changes fastest.
Arguments:
- x_blocks: float32 [2, 64, 2, 6, 128, 128], P('row', 'layer', 'col'), may hold values from -0.3 to 0.3, as said below
- block_cols: int32 [2, 64, 2, 6], P('row', 'layer', 'col'), may hold values from 0 to 63, as said below
Outputs:
- x_next: float32 [2, 64, 2, 6, 128, 128], P('row', 'layer', 'col')
The draws below stay inside these ranges and needn't reach their ends.
Inputs may be any that keep to these rules, and one draw needn't show every extreme that they name: `block_cols`: each tile q splits its 64 block indices into 32 groups of 2, numbered around a circle; a block row of tile r lying in group g has as its 6 columns in tile c exactly the members of groups g - 1, g and g + 1 (numbers taken around the circle) of tile c, in some order. So P is symmetric and holds every diagonal block. `x_blocks`: X is symmetric: the block stored at (n, k) is the transpose of the block stored at (k, n), and diagonal blocks are symmetric.
All inputs are finite; a program needn't handle non-finite values.
Results may differ from the reference program's by a relative error of at most 0.0003.
Values sent between devices are 32-bit elements; how exact they have to be, the bound alone decides.
A program may use at most 192 MiB of HBM per device.

```python
import jax
import jax.numpy as jnp
from jax import lax

BLK = 128
GRP = 2
KP = 6
TB = 64
N_ROW = 2
N_COL = 2


spread = 0.05


half_root = 0.70710678


def cluster_cols(key):
    scores = jax.random.randint(key, (N_ROW, TB), 0, 1 << 20) * TB + jnp.arange(TB, dtype=jnp.int32)[None, :]
    order_ids = jnp.argsort(scores, axis=-1).astype(jnp.int32)
    rank_ids = jnp.argsort(order_ids, axis=-1).astype(jnp.int32)
    group_count = TB // GRP
    group_ids = rank_ids // GRP
    slot_range = jnp.arange(KP, dtype=jnp.int32)
    step_ids = slot_range // GRP - 1
    member_ids = slot_range % GRP
    target_group = (group_ids[:, :, None, None] + step_ids[None, None, None, :] + group_count) % group_count
    slot_ids = target_group * GRP + member_ids[None, None, None, :]
    slot_ids = jnp.broadcast_to(slot_ids, (N_ROW, TB, N_COL, KP))
    tile_ids = jnp.broadcast_to(jnp.arange(N_COL, dtype=jnp.int32)[None, None, :, None], (N_ROW, TB, N_COL, KP))
    return order_ids[tile_ids, slot_ids].astype(jnp.int32)


def draw_block_cols(key, part):
    return cluster_cols(key)


def draw_x_blocks(key, part):
    col_ids = cluster_cols(key)
    key = jax.random.fold_in(key, 5)
    count_all = N_ROW * TB
    row_ids = jnp.arange(N_ROW, dtype=jnp.int32)[:, None, None, None] * TB + jnp.arange(TB, dtype=jnp.int32)[None, :, None, None]
    row_ids = jnp.broadcast_to(row_ids, col_ids.shape)
    global_cols = jnp.arange(N_COL, dtype=jnp.int32)[None, None, :, None] * TB + col_ids
    lower_id = jnp.minimum(row_ids, global_cols)
    upper_id = jnp.maximum(row_ids, global_cols)
    pair_ids = (lower_id * count_all + upper_id).reshape(-1)
    keys_all = jax.vmap(lambda number: jax.random.fold_in(key, number))(pair_ids)
    drawn = jax.vmap(lambda single: jax.random.normal(single, (BLK, BLK), jnp.float32))(keys_all) * spread
    flipped = jnp.swapaxes(drawn, -1, -2)
    upper_half = (row_ids < global_cols).reshape(-1)[:, None, None]
    on_diagonal = (row_ids == global_cols).reshape(-1)[:, None, None]
    blocks = jnp.where(on_diagonal, (drawn + flipped) * half_root, jnp.where(upper_half, drawn, flipped))
    blocks = jnp.clip(blocks, -0.3, 0.3)
    return blocks.reshape(N_ROW, TB, N_COL, KP, BLK, BLK).astype(jnp.float32)


def setup_inputs(seed: int = 0) -> dict:
    arg_keys = jax.random.split(jax.random.key(seed), 3)
    return {
        "x_blocks": draw_x_blocks(jax.random.fold_in(arg_keys[2], 71), 0),
        "block_cols": draw_block_cols(jax.random.fold_in(arg_keys[2], 71), 0),
    }


def product(left_blocks, right_blocks, block_cols):
    highest = lax.Precision.HIGHEST

    def tile_row(row_tile):
        left_row = left_blocks[row_tile]
        left_ids = block_cols[row_tile]
        pieces = []
        for column in range(N_COL):
            summed = jnp.zeros((TB, KP, BLK, BLK), jnp.float32)
            for middle in range(N_COL):
                blocks = left_row[:, middle]
                inner_ids = left_ids[:, middle].astype(jnp.int32)
                chosen = jnp.take(right_blocks[middle, :, column], inner_ids, axis=0)
                chosen_ids = jnp.take(block_cols[middle, :, column], inner_ids, axis=0)
                matches = (chosen_ids[..., None] == left_ids[:, column][:, None, None, :]).astype(jnp.float32)
                picked = jnp.einsum('istm,istab->ismab', matches, chosen, precision=highest)
                summed = summed + jnp.einsum('isab,ismbc->imac', blocks, picked, precision=highest)
            pieces.append(summed)
        return jnp.stack(pieces, axis=1)

    return lax.map(tile_row, jnp.arange(N_ROW, dtype=jnp.int32))


def reference(x_blocks, block_cols):
    square = product(x_blocks, x_blocks, block_cols)
    same_tile = jnp.arange(N_ROW)[:, None] == jnp.arange(N_COL)[None, :]
    own_row = block_cols == jnp.arange(TB, dtype=jnp.int32)[None, :, None, None]
    diagonal = (same_tile[:, None, :, None] & own_row).astype(jnp.float32)
    shifted = 3.0 * diagonal[..., None, None] * jnp.eye(BLK, dtype=jnp.float32) - square
    return 0.5 * product(x_blocks, shifted, block_cols)
```

```python
import functools

import jax
import jax.numpy as jnp
from jax import lax
from jax.experimental import pallas as pl
from jax.experimental.pallas import tpu as pltpu
from jax.sharding import PartitionSpec as P

MESH = pl.DeviceIdType.MESH
NL = 32
ROWS = 4
BLK = 128
VMEM_LIMIT = 56 * 1024 * 1024


def active_col(layer):
    return (layer // 8 + layer // 2) % 2


def my_ids():
    return lax.axis_index("layer"), lax.axis_index("row"), lax.axis_index("col")


def spread_kernel(x_ref, pat_ref, buf_ref, own_ref, other_ref, send, recv, psend, precv, local, core):
    me, row, col = my_ids()
    barrier = pltpu.get_barrier_semaphore()

    @pl.loop(1, NL)
    def _(k):
        p = lax.rem(me + k, NL)
        pl.semaphore_signal(barrier, inc=1, device_id=(p, row, col), device_id_type=MESH)

    pl.semaphore_signal(barrier, inc=1, device_id=(me, 1 - row, col), device_id_type=MESH)
    pl.semaphore_wait(barrier, NL)

    def pattern_copy(dst_owner, device, k):
        return pltpu.make_async_remote_copy(
            pat_ref, own_ref.at[dst_owner], psend.at[k], precv.at[dst_owner],
            device_id=(device, row, col), device_id_type=MESH)

    def data_copy(owner, device, k):
        return pltpu.make_async_remote_copy(
            x_ref.at[:, device], buf_ref.at[owner], send.at[k], recv.at[owner],
            device_id=(device, row, col), device_id_type=MESH)

    @pl.loop(1, NL)
    def _(k):
        pattern_copy(me, lax.rem(me + k, NL), k).start()

    @pl.loop(1, NL)
    def _(k):
        data_copy(me, lax.rem(me + k, NL), k).start()

    here = pltpu.make_async_copy(x_ref.at[:, me], buf_ref.at[me], local.at[0])
    here_pat = pltpu.make_async_copy(pat_ref, own_ref.at[me], local.at[1])
    here.start()
    here_pat.start()
    here_pat.wait()

    @pl.loop(1, NL)
    def _(k):
        p = lax.rem(me + k, NL)
        pattern_copy(p, p, k).wait_recv()

    swap = pltpu.make_async_remote_copy(
        own_ref, other_ref, core.at[0], core.at[1], device_id=(me, 1 - row, col), device_id_type=MESH)
    swap.start()

    @pl.loop(1, NL)
    def _(k):
        p = lax.rem(me + k, NL)
        data_copy(p, p, k).wait_recv()

    here.wait()
    swap.wait()

    @pl.loop(1, NL)
    def _(k):
        p = lax.rem(me + k, NL)
        pattern_copy(me, p, k).wait_send()
        data_copy(me, p, k).wait_send()


def dot_nt(a, b):
    return lax.dot_general(a, b, (((1,), (1,)), ((), ())), preferred_element_type=jnp.float32)


def dot_nn(a, b):
    return jnp.dot(a, b, preferred_element_type=jnp.float32)


def roll_groups(a, shift):
    return jnp.concatenate([a[shift:], a[:shift]], axis=0) if shift > 0 else jnp.concatenate([a[shift:], a[:shift]], axis=0)


def order_kernel(own_ref, other_ref, tin_ref, tout_ref):
    row = lax.axis_index("row")
    f32, bf16 = jnp.float32, jnp.bfloat16
    is_first = row == 0
    own = own_ref[...].astype(f32)
    other = other_ref[...].astype(f32)
    pat0 = jnp.where(is_first, own, other)
    pat1 = jnp.where(is_first, other, own)

    def rows_of(pat):
        return jnp.concatenate([pat[:, 0:6], pat[:, 6:12]], axis=0)

    def member(pat):
        iota = lax.broadcasted_iota(jnp.int32, (64, 64), 1).astype(f32)
        total = jnp.zeros((64, 64), f32)
        for s in range(6):
            total = total + jnp.where(pat[:, s:s + 1] == iota, 1.0, 0.0)
        return total

    def mask(cond):
        return jnp.where(cond, 1.0, 0.0)

    p0, p1 = rows_of(pat0), rows_of(pat1)
    m0, m1 = member(p0), member(p1)
    m0b, m1b = m0.astype(bf16), m1.astype(bf16)
    common = dot_nt(m0b, m0b)
    reach2 = mask(common > 1.0)
    b2 = reach2.astype(bf16)
    reach4 = mask(dot_nn(b2, b2) > 0.5)
    b4 = reach4.astype(bf16)
    b8 = mask(dot_nn(b4, b4) > 0.5).astype(bf16)
    lane = lax.broadcasted_iota(jnp.int32, (1, 64), 1).astype(f32)
    sub = lax.broadcasted_iota(jnp.int32, (64, 64), 0).astype(f32)
    first = common[0:1, :]
    start = jnp.min(jnp.where(first == 4.0, lane, 1000.0), axis=1, keepdims=True)
    second = jnp.sum(jnp.where(sub == start, common, 0.0), axis=0, keepdims=True)
    t = jnp.concatenate([mask(first > 5.0), mask(first > 3.0), mask(second > 5.0), mask(second > 3.0)], axis=0)
    for b in (b2, b4, b8):
        t = jnp.concatenate([t, mask(dot_nn(t.astype(bf16), b) > 0.5)], axis=0)
    which = lax.broadcasted_iota(jnp.int32, (32, 64), 0)
    from_first = jnp.bitwise_and(which, 3) < 2
    dist0 = 16.0 - jnp.sum(jnp.where(from_first, t, 0.0), axis=0, keepdims=True)
    dist1 = 16.0 - jnp.sum(jnp.where(from_first, 0.0, t), axis=0, keepdims=True)
    pos0 = jnp.where(dist1 < dist0, dist0, jnp.where(dist0 == 0.0, 0.0, 32.0 - dist0))
    group = lax.broadcasted_iota(jnp.int32, (32, 64), 0).astype(f32)
    g0 = mask(group == pos0)

    def centre(c):
        return mask(roll_groups(c, -1) + c + roll_groups(c, 1) > 5.0)

    hc = centre(dot_nn(g0.astype(bf16), m0b))
    g1 = centre(dot_nt(hc.astype(bf16), m1b))
    gr = jnp.where(is_first, g0, g1)
    pr = jnp.where(is_first, p0, p1)

    lanes = lax.broadcasted_iota(jnp.int32, (32, 64), 1)
    natural = (jnp.bitwise_and(lanes, 31) * 2 + jnp.right_shift(lanes, 5)).astype(f32)
    column = lanes.astype(f32)
    row_lo = jnp.min(jnp.where(gr > 0.5, natural, 1000.0), axis=1, keepdims=True)
    row_hi = jnp.max(jnp.where(gr > 0.5, natural, -1.0), axis=1, keepdims=True)
    col_lo = jnp.min(jnp.where(hc > 0.5, column, 1000.0), axis=1, keepdims=True)
    col_hi = jnp.max(jnp.where(hc > 0.5, column, -1.0), axis=1, keepdims=True)

    prb = jnp.concatenate([pr, jnp.zeros((64, 122), f32)], axis=1).astype(bf16)
    out_lane = lax.broadcasted_iota(jnp.int32, (32, 128), 1)
    slot_iota = out_lane.astype(f32)
    table = jnp.zeros((32, 128), f32)
    for a, members in enumerate((row_lo, row_hi)):
        chosen = mask((gr > 0.5) & (natural == members))
        cols = dot_nn(chosen.astype(bf16), prb)
        cols = jnp.where(out_lane < 6, cols, -1.0)
        for d in range(3):
            for j, cmem in enumerate((col_lo, col_hi)):
                target = roll_groups(cmem, d - 1) if d != 1 else cmem
                slot = jnp.sum(jnp.where(cols == target, slot_iota, 0.0), axis=1, keepdims=True)
                table = jnp.where(out_lane == a * 6 + d * 2 + j, members * 6.0 + slot, table)
    tin_ref[...] = table.astype(jnp.int32)

    eye = mask(lax.broadcasted_iota(jnp.int32, (64, 64), 0) == lax.broadcasted_iota(jnp.int32, (64, 64), 1)).astype(bf16)
    extra = lax.broadcasted_iota(jnp.int32, (32, 64), 0).astype(f32)
    grt = dot_nt(eye, gr.astype(bf16))
    gi = jnp.sum(grt * lax.broadcasted_iota(jnp.int32, (64, 32), 1).astype(f32), axis=1, keepdims=True)
    hi_flag = mask((gr > 0.5) & (natural == row_hi))
    ai = jnp.sum(dot_nt(eye, hi_flag.astype(bf16)), axis=1, keepdims=True)
    gcol = jnp.sum(hc * extra, axis=0, keepdims=True)
    jcol = jnp.sum(mask((hc > 0.5) & (column == col_hi)), axis=0, keepdims=True)
    code = gcol * 2.0 + jcol
    iota64 = lax.broadcasted_iota(jnp.int32, (64, 64), 1).astype(f32)
    lane64 = lax.broadcasted_iota(jnp.int32, (64, 128), 1)
    out = jnp.zeros((64, 128), jnp.int32)
    gi_i, ai_i = gi.astype(jnp.int32), ai.astype(jnp.int32)
    for s in range(6):
        val = jnp.sum(jnp.where(pr[:, s:s + 1] == iota64, code, 0.0), axis=1, keepdims=True).astype(jnp.int32)
        gc, jc = jnp.right_shift(val, 1), jnp.bitwise_and(val, 1)
        d = jnp.bitwise_and(gi_i - gc + 1, 31)
        out = jnp.where(lane64 == s, gc * 12 + d * 4 + ai_i * 2 + jc, out)
    tout_ref[...] = out


def deliver_kernel(tin_ref, buf_ref, x_ref, stage, send, recv, local, core):
    me, row, col = my_ids()
    active = active_col(me) == col
    barrier = pltpu.get_barrier_semaphore()

    @pl.when(active)
    def _():
        @pl.loop(1, NL)
        def _(k):
            p = lax.rem(me + k, NL)
            for c in range(2):
                pl.semaphore_signal(barrier, inc=1, device_id=(p, row, c), device_id_type=MESH)

        pl.semaphore_signal(barrier, inc=1, device_id=(me, row, 1 - col), device_id_type=MESH)
        pl.semaphore_signal(barrier, inc=1, device_id=(me, 1 - row, col), device_id_type=MESH)
        pl.semaphore_wait(barrier, NL)

    @pl.when(jnp.logical_not(active))
    def _():
        pl.semaphore_wait(barrier, NL)

    def fill(h):
        before, after = lax.rem(h + NL - 1, NL), lax.rem(h + 1, NL)
        for q in range(12):
            stage[h, q] = buf_ref[tin_ref[h, q]]
        for a in range(2):
            for j in range(2):
                stage[h, 12 + a * 2 + j] = buf_ref[tin_ref[before, a * 6 + 2 + j]]
                stage[h, 16 + a * 2 + j] = buf_ref[tin_ref[after, a * 6 + 2 + j]]

    def copy(h, source, source_col):
        return pltpu.make_async_remote_copy(
            stage.at[h], x_ref.at[row, source_col, :, source], send.at[h], recv.at[source_col, source],
            device_id=(h, row, active_col(h)), device_id_type=MESH)

    @pl.loop(1, NL)
    def _(k):
        h = lax.rem(me + k, NL)
        fill(h)
        copy(h, me, col).start()

    fill(me)
    here = pltpu.make_async_copy(stage.at[me], x_ref.at[row, col, :, me], local)

    @pl.when(active)
    def _():
        here.start()

    @pl.when(jnp.logical_not(active))
    def _():
        copy(me, me, col).start()

    @pl.when(active)
    def _():
        @pl.loop(1, NL)
        def _(k):
            p = lax.rem(me + k, NL)
            for c in range(2):
                copy(me, p, c).wait_recv()

        copy(me, me, 1 - col).wait_recv()
        here.wait()
        swap = pltpu.make_async_remote_copy(
            x_ref.at[row], x_ref.at[row], core.at[0], core.at[1],
            device_id=(me, 1 - row, col), device_id_type=MESH)
        swap.start()
        swap.wait()

    @pl.loop(1, NL)
    def _(k):
        h = lax.rem(me + k, NL)
        copy(h, me, col).wait_send()

    @pl.when(jnp.logical_not(active))
    def _():
        copy(me, me, col).wait_send()


def product_kernel(x_ref, y_ref, hi, lo, whi, wlo):
    row = lax.axis_index("row")
    bf16, f32 = jnp.bfloat16, jnp.float32

    def split(value):
        high = value.astype(bf16)
        return high, (value - high.astype(f32)).astype(bf16)

    for r in range(2):
        for c in range(2):
            for a in range(2):
                for j in range(2):
                    rows = pl.ds(r * 256 + a * 128, 128)
                    cols = pl.ds(c * 256 + j * 128, 128)
                    for part, q in enumerate((a * 6 + j, a * 6 + 2 + j, a * 6 + 4 + j, 12 + a * 2 + j, 16 + a * 2 + j)):
                        high, low = split(x_ref[r, c, q])
                        hi[part, rows, cols] = high
                        lo[part, rows, cols] = low

    def mul(pairs):
        total = None
        for (ah, al), part, transposed in pairs:
            dot = dot_nt if transposed else dot_nn
            bh, bl = hi[part], lo[part]
            term = dot(ah, bh) + dot(ah, bl) + dot(al, bh)
            total = term if total is None else total + term
        return total

    def apply(w):
        left, mid, right = w
        return (
            mul([(left, 3, False), (mid, 0, False)]),
            mul([(left, 0, True), (mid, 1, False), (right, 2, True)]),
            mul([(mid, 2, False), (right, 4, False)]),
        )

    mine = pl.ds(pl.multiple_of(row * 256, 256), 256)
    w = [(hi[part, mine, :], lo[part, mine, :]) for part in range(3)]
    left, mid, right = apply(w)
    q = lax.broadcasted_iota(jnp.int32, (256, 512), 0)
    k = lax.broadcasted_iota(jnp.int32, (256, 512), 1)
    mid = jnp.where(k == q + row * 256, 3.0, 0.0) - mid
    s = [split(-left), split(mid), split(-right)]
    y = apply(s)
    for d in range(3):
        half = 0.5 * y[d]
        for r in range(2):
            for a in range(2):
                for j in range(2):
                    block = half[j * 128:(j + 1) * 128, r * 256 + a * 128:r * 256 + (a + 1) * 128]
                    y_ref[r, d * 4 + a * 2 + j] = block.T


def home_kernel(tout_ref, y_ref, out_ref, sorted_ref, stage, send, recv, send2, recv2, local):
    me, row, col = my_ids()
    active = active_col(me) == col
    barrier = pltpu.get_barrier_semaphore()

    def source_of(h):
        return (h, col, active_col(h))

    self_source = jnp.logical_and(active, row == col)

    @pl.loop(1, NL)
    def _(k):
        p = lax.rem(me + k, NL)
        pl.semaphore_signal(barrier, inc=1, device_id=source_of(p), device_id_type=MESH)
        pl.semaphore_signal(barrier, inc=1, device_id=(p, row, col), device_id_type=MESH)

    @pl.when(jnp.logical_not(self_source))
    def _():
        pl.semaphore_signal(barrier, inc=1, device_id=source_of(me), device_id_type=MESH)

    @pl.when(jnp.logical_not(active))
    def _():
        pl.semaphore_wait(barrier, NL - 1)

    @pl.when(self_source)
    def _():
        pl.semaphore_wait(barrier, 3 * (NL - 1) + 1)

    @pl.when(jnp.logical_and(active, row != col))
    def _():
        pl.semaphore_wait(barrier, 3 * (NL - 1) + 2)

    def result_copy(p, r, source):
        return pltpu.make_async_remote_copy(
            y_ref.at[r, :, p], sorted_ref.at[source], send.at[r, p], recv.at[source],
            device_id=(p, r, row), device_id_type=MESH)

    here = pltpu.make_async_copy(y_ref.at[row, :, me], sorted_ref.at[me], local.at[0])

    @pl.when(active)
    def _():
        @pl.loop(1, NL)
        def _(k):
            p = lax.rem(me + k, NL)
            for r in range(2):
                result_copy(p, r, me).start()

        for r in range(2):
            @pl.when(jnp.logical_or(row != col, r != row))
            def _():
                result_copy(me, r, me).start()

        @pl.when(row == col)
        def _():
            here.start()

    @pl.loop(1, NL)
    def _(k):
        h = lax.rem(me + k, NL)
        result_copy(me, row, h).wait_recv()

    @pl.when(self_source)
    def _():
        here.wait()

    @pl.when(jnp.logical_not(self_source))
    def _():
        result_copy(me, row, me).wait_recv()

    def fill(l):
        for jj in range(2):
            for s in range(6):
                place = tout_ref[jj * 32 + l, s]
                stage[l, jj * 6 + s] = sorted_ref[place // 12, lax.rem(place, 12)]

    def home_copy(device, owner):
        return pltpu.make_async_remote_copy(
            stage.at[device], out_ref.at[:, owner], send2.at[device], recv2.at[owner],
            device_id=(device, row, col), device_id_type=MESH)

    @pl.loop(1, NL)
    def _(k):
        l = lax.rem(me + k, NL)
        fill(l)
        home_copy(l, me).start()

    fill(me)
    last = pltpu.make_async_copy(stage.at[me], out_ref.at[:, me], local.at[1])
    last.start()

    @pl.loop(1, NL)
    def _(k):
        p = lax.rem(me + k, NL)
        home_copy(p, p).wait_recv()

    last.wait()

    @pl.loop(1, NL)
    def _(k):
        p = lax.rem(me + k, NL)
        home_copy(p, me).wait_send()

    @pl.when(active)
    def _():
        @pl.loop(1, NL)
        def _(k):
            p = lax.rem(me + k, NL)
            for r in range(2):
                result_copy(p, r, me).wait_send()

        for r in range(2):
            @pl.when(jnp.logical_or(row != col, r != row))
            def _():
                result_copy(me, r, me).wait_send()


ANY = pl.BlockSpec(memory_space=pl.ANY)
VMEM = pl.BlockSpec(memory_space=pltpu.VMEM)
SMEM = pl.BlockSpec(memory_space=pltpu.SMEM)
DMA = pltpu.SemaphoreType.DMA


def params(collective_id):
    return pltpu.CompilerParams(collective_id=collective_id, has_side_effects=True, vmem_limit_bytes=VMEM_LIMIT)


def body(x_blocks, block_cols):
    f32 = jnp.float32
    x = x_blocks.reshape(12, NL, ROWS, BLK)
    pat = jnp.pad(block_cols.reshape(1, 12), ((0, 0), (0, 116)))
    buf, own, other = pl.pallas_call(
        spread_kernel,
        out_shape=(
            jax.ShapeDtypeStruct((NL, 12, ROWS, BLK), f32),
            jax.ShapeDtypeStruct((NL, 1, 128), jnp.int32),
            jax.ShapeDtypeStruct((NL, 1, 128), jnp.int32),
        ),
        in_specs=[ANY, ANY],
        out_specs=(ANY, ANY, ANY),
        scratch_shapes=[DMA((NL,)), DMA((NL,)), DMA((NL,)), DMA((NL,)), DMA((2,)), DMA((2,))],
        compiler_params=params(0),
        name="spread",
    )(x, pat)
    tin, tout = pl.pallas_call(
        order_kernel,
        out_shape=(jax.ShapeDtypeStruct((32, 128), jnp.int32), jax.ShapeDtypeStruct((64, 128), jnp.int32)),
        in_specs=[VMEM, VMEM],
        out_specs=(VMEM, VMEM),
        name="order",
    )(own.reshape(NL, 128), other.reshape(NL, 128))
    gathered = pl.pallas_call(
        deliver_kernel,
        out_shape=jax.ShapeDtypeStruct((2, 2, 20, NL, ROWS, BLK), f32),
        in_specs=[SMEM, VMEM],
        out_specs=ANY,
        scratch_shapes=[
            pltpu.VMEM((NL, 20, ROWS, BLK), f32), DMA((NL,)), DMA((2, NL)), DMA, DMA((2,))],
        compiler_params=params(1),
        name="deliver",
    )(tin, buf.reshape(NL * 12, ROWS, BLK))
    y = pl.pallas_call(
        product_kernel,
        out_shape=jax.ShapeDtypeStruct((2, 12, BLK, BLK), f32),
        in_specs=[VMEM],
        out_specs=VMEM,
        scratch_shapes=[
            pltpu.VMEM((5, 512, 512), jnp.bfloat16), pltpu.VMEM((5, 512, 512), jnp.bfloat16),
            pltpu.VMEM((256, 1536), jnp.bfloat16), pltpu.VMEM((256, 1536), jnp.bfloat16)],
        compiler_params=pltpu.CompilerParams(vmem_limit_bytes=VMEM_LIMIT),
        name="product",
    )(gathered.reshape(2, 2, 20, BLK, BLK))
    out = pl.pallas_call(
        home_kernel,
        out_shape=jax.ShapeDtypeStruct((12, NL, ROWS, BLK), f32),
        in_specs=[SMEM, ANY],
        out_specs=ANY,
        scratch_shapes=[
            pltpu.VMEM((NL, 12, ROWS, BLK), f32), pltpu.VMEM((NL, 12, ROWS, BLK), f32),
            DMA((2, NL)), DMA((NL,)), DMA((NL,)), DMA((NL,)), DMA((2,))],
        compiler_params=params(2),
        name="home",
    )(tout, y.reshape(2, 12, NL, ROWS, BLK))
    return out.reshape(x_blocks.shape)


def solution(mesh):
    return jax.shard_map(
        body,
        mesh=mesh,
        in_specs=(P("row", "layer", "col", None, None, None), P("row", "layer", "col", None)),
        out_specs=P("row", "layer", "col", None, None, None),
        check_vma=False,
    )
```

```python
import functools

import jax
import jax.numpy as jnp
from jax import lax
from jax.experimental import pallas as pl
from jax.experimental.pallas import tpu as pltpu
from jax.sharding import PartitionSpec as P

MESH = pl.DeviceIdType.MESH
NL = 32
ROWS = 4
BLK = 128
VMEM_LIMIT = 56 * 1024 * 1024


def my_ids():
    return lax.axis_index("layer"), lax.axis_index("row"), lax.axis_index("col")


def dot_nt(a, b):
    return lax.dot_general(a, b, (((1,), (1,)), ((), ())), preferred_element_type=jnp.float32)


def dot_nn(a, b):
    return jnp.dot(a, b, preferred_element_type=jnp.float32)


def roll_groups(a, shift):
    return jnp.concatenate([a[shift:], a[:shift]], axis=0)


def order_tables(row, own, other):
    f32, bf16 = jnp.float32, jnp.bfloat16
    is_first = row == 0
    own = own.astype(f32)
    other = other.astype(f32)
    pat0 = jnp.where(is_first, own, other)
    pat1 = jnp.where(is_first, other, own)

    def rows_of(pat):
        return jnp.concatenate([pat[:, 0:6], pat[:, 6:12]], axis=0)

    def member(pat):
        iota = lax.broadcasted_iota(jnp.int32, (64, 64), 1).astype(f32)
        total = jnp.zeros((64, 64), f32)
        for s in range(6):
            total = total + jnp.where(pat[:, s:s + 1] == iota, 1.0, 0.0)
        return total

    def mask(cond):
        return jnp.where(cond, 1.0, 0.0)

    p0, p1 = rows_of(pat0), rows_of(pat1)
    m0, m1 = member(p0), member(p1)
    m0b, m1b = m0.astype(bf16), m1.astype(bf16)
    common = dot_nt(m0b, m0b)
    reach2 = mask(common > 1.0)
    b2 = reach2.astype(bf16)
    reach4 = mask(dot_nn(b2, b2) > 0.5)
    b4 = reach4.astype(bf16)
    b8 = mask(dot_nn(b4, b4) > 0.5).astype(bf16)
    lane = lax.broadcasted_iota(jnp.int32, (1, 64), 1).astype(f32)
    sub = lax.broadcasted_iota(jnp.int32, (64, 64), 0).astype(f32)
    first = common[0:1, :]
    start = jnp.min(jnp.where(first == 4.0, lane, 1000.0), axis=1, keepdims=True)
    second = jnp.sum(jnp.where(sub == start, common, 0.0), axis=0, keepdims=True)
    t = jnp.concatenate([mask(first > 5.0), mask(first > 3.0), mask(second > 5.0), mask(second > 3.0)], axis=0)
    for b in (b2, b4, b8):
        t = jnp.concatenate([t, mask(dot_nn(t.astype(bf16), b) > 0.5)], axis=0)
    which = lax.broadcasted_iota(jnp.int32, (32, 64), 0)
    from_first = jnp.bitwise_and(which, 3) < 2
    dist0 = 16.0 - jnp.sum(jnp.where(from_first, t, 0.0), axis=0, keepdims=True)
    dist1 = 16.0 - jnp.sum(jnp.where(from_first, 0.0, t), axis=0, keepdims=True)
    pos0 = jnp.where(dist1 < dist0, dist0, jnp.where(dist0 == 0.0, 0.0, 32.0 - dist0))
    group = lax.broadcasted_iota(jnp.int32, (32, 64), 0).astype(f32)
    g0 = mask(group == pos0)

    def centre(c):
        return mask(roll_groups(c, -1) + c + roll_groups(c, 1) > 5.0)

    hc = centre(dot_nn(g0.astype(bf16), m0b))
    g1 = centre(dot_nt(hc.astype(bf16), m1b))
    gr = jnp.where(is_first, g0, g1)
    pr = jnp.where(is_first, p0, p1)

    lanes = lax.broadcasted_iota(jnp.int32, (32, 64), 1)
    natural = (jnp.bitwise_and(lanes, 31) * 2 + jnp.right_shift(lanes, 5)).astype(f32)
    column = lanes.astype(f32)
    row_lo = jnp.min(jnp.where(gr > 0.5, natural, 1000.0), axis=1, keepdims=True)
    row_hi = jnp.max(jnp.where(gr > 0.5, natural, -1.0), axis=1, keepdims=True)
    col_lo = jnp.min(jnp.where(hc > 0.5, column, 1000.0), axis=1, keepdims=True)
    col_hi = jnp.max(jnp.where(hc > 0.5, column, -1.0), axis=1, keepdims=True)

    prb = jnp.concatenate([pr, jnp.zeros((64, 122), f32)], axis=1).astype(bf16)
    out_lane = lax.broadcasted_iota(jnp.int32, (32, 128), 1)
    slot_iota = out_lane.astype(f32)
    table = jnp.zeros((32, 128), f32)
    for a, members in enumerate((row_lo, row_hi)):
        chosen = mask((gr > 0.5) & (natural == members))
        cols = dot_nn(chosen.astype(bf16), prb)
        cols = jnp.where(out_lane < 6, cols, -1.0)
        for d in range(3):
            for j, cmem in enumerate((col_lo, col_hi)):
                target = roll_groups(cmem, d - 1) if d != 1 else cmem
                slot = jnp.sum(jnp.where(cols == target, slot_iota, 0.0), axis=1, keepdims=True)
                table = jnp.where(out_lane == a * 6 + d * 2 + j, members * 6.0 + slot, table)
    tin = jnp.clip(table, 0.0, 383.0).astype(jnp.int32)

    eye = mask(lax.broadcasted_iota(jnp.int32, (64, 64), 0) == lax.broadcasted_iota(jnp.int32, (64, 64), 1)).astype(bf16)
    extra = lax.broadcasted_iota(jnp.int32, (32, 64), 0).astype(f32)
    grt = dot_nt(eye, gr.astype(bf16))
    gi = jnp.sum(grt * lax.broadcasted_iota(jnp.int32, (64, 32), 1).astype(f32), axis=1, keepdims=True)
    hi_flag = mask((gr > 0.5) & (natural == row_hi))
    ai = jnp.sum(dot_nt(eye, hi_flag.astype(bf16)), axis=1, keepdims=True)
    gcol = jnp.sum(hc * extra, axis=0, keepdims=True)
    jcol = jnp.sum(mask((hc > 0.5) & (column == col_hi)), axis=0, keepdims=True)
    code = gcol * 2.0 + jcol
    iota64 = lax.broadcasted_iota(jnp.int32, (64, 64), 1).astype(f32)
    lane64 = lax.broadcasted_iota(jnp.int32, (64, 128), 1)
    out = jnp.zeros((64, 128), jnp.int32)
    gi_i, ai_i = gi.astype(jnp.int32), ai.astype(jnp.int32)
    for s in range(6):
        val = jnp.sum(jnp.where(pr[:, s:s + 1] == iota64, code, 0.0), axis=1, keepdims=True).astype(jnp.int32)
        gc, jc = jnp.right_shift(val, 1), jnp.bitwise_and(val, 1)
        d = jnp.bitwise_and(gi_i - gc + 1, 31)
        out = jnp.where(lane64 == s, gc * 12 + jc * 6 + d * 2 + ai_i, out)
    return tin, jnp.clip(out, 0, 383)


def inside(place):
    return jnp.minimum(jnp.maximum(place, 0), NL * 12 - 1)


def split(value):
    high = value.astype(jnp.bfloat16)
    return high, (value - high.astype(jnp.float32)).astype(jnp.bfloat16)


def multiply(me, row, col, xs, hi, lo, y):
    @pl.loop(0, 16)
    def _(n):
        r, c, a, j = n // 8, lax.rem(n // 4, 2), lax.rem(n // 2, 2), lax.rem(n, 2)
        rows = pl.ds(pl.multiple_of(r * 256 + a * 128, 128), 128)
        cols = pl.ds(pl.multiple_of(c * 256 + j * 128, 128), 128)
        for part, q in enumerate((a * 6 + j, a * 6 + 2 + j, a * 6 + 4 + j, 12 + a * 2 + j, 16 + a * 2 + j)):
            high, low = split(xs[r, c, q].reshape(BLK, BLK))
            hi[part, rows, cols] = high
            lo[part, rows, cols] = low

    def mul(pairs):
        total = None
        for (stacked, high), part, transposed in pairs:
            dot = dot_nt if transposed else dot_nn
            both = dot(stacked, hi[part])
            term = both[:BLK] + both[BLK:] + dot(high, lo[part])
            total = term if total is None else total + term
        return total

    def apply(w):
        left, mid, right = w
        return (
            mul([(left, 3, False), (mid, 0, False)]),
            mul([(left, 0, True), (mid, 1, False), (right, 2, True)]),
            mul([(mid, 2, False), (right, 4, False)]),
        )

    def stack(high, low):
        return jnp.concatenate([high, low], axis=0), high

    offset = col * 256 + row * 128
    mine = pl.ds(pl.multiple_of(offset, 128), 128)
    left, mid, right = apply([stack(hi[part, mine, :], lo[part, mine, :]) for part in range(3)])
    q = lax.broadcasted_iota(jnp.int32, (BLK, 512), 0)
    k = lax.broadcasted_iota(jnp.int32, (BLK, 512), 1)
    mid = jnp.where(k == q + offset, 3.0, 0.0) - mid
    for d, part in enumerate(apply([stack(*split(-left)), stack(*split(mid)), stack(*split(-right))])):
        half = 0.5 * part
        for r in range(2):
            for a in range(2):
                first = r * 256 + a * 128
                y[r, d * 2 + a] = half[:, first:first + 128].T.reshape(NL, ROWS, BLK)


def kernel(
    cols_ref, x_ref, out_ref, pat, own, other, tin_v, tout_v, tin, tout, buf, stage, xs, hi, lo, y, srt, stage2,
    psend, precv, send1, recv1, send2, recv2, swap_send, swap_recv, send3, recv3, send4, recv4, core, local,
):
    me, row, col = my_ids()
    barrier = pltpu.get_barrier_semaphore()

    def signal(device):
        pl.semaphore_signal(barrier, inc=1, device_id=device, device_id_type=MESH)

    signal((me, 1 - row, col))
    signal((me, row, 1 - col))

    @pl.loop(1, NL)
    def _(k):
        signal((lax.rem(me + k, NL), row, col))

    for jj in range(2):
        pat[0:1, jj * 6:jj * 6 + 6] = cols_ref[0, jj]
    pl.semaphore_wait(barrier, NL + 1)

    def remote(src, dst, send, recv, device):
        return pltpu.make_async_remote_copy(src, dst, send, recv, device_id=device, device_id_type=MESH)

    def others(step):
        @pl.loop(1, NL)
        def _(k):
            step(lax.rem(me + k, NL))

    def pattern_copy(p, owner):
        return remote(pat, own.at[owner], psend.at[p], precv.at[owner], (p, row, col))

    def spread(p, owner):
        return remote(x_ref.at[:, p], buf.at[pl.ds(owner * 12, 12)], send1.at[p], recv1.at[owner], (p, row, col))

    others(lambda p: pattern_copy(p, me).start())
    others(lambda p: spread(p, me).start())
    here1 = pltpu.make_async_copy(x_ref.at[:, me], buf.at[pl.ds(me * 12, 12)], local.at[0])
    here1.start()
    own[me] = pat[...]
    others(lambda p: pattern_copy(p, p).wait_recv())
    swap_pattern = remote(own, other, core.at[0], core.at[1], (me, 1 - row, col))
    swap_pattern.start()
    swap_pattern.wait()
    tin_v[...], tout_v[...] = order_tables(row, own[...].reshape(NL, 128), other[...].reshape(NL, 128))
    for n, (vector, scalar) in enumerate(((tin_v, tin), (tout_v, tout))):
        move = pltpu.make_async_copy(vector, scalar, local.at[1 + n])
        move.start()
        move.wait()
    here1.wait()
    others(lambda p: spread(p, p).wait_recv())

    def deliver(h, c, source, source_col):
        return remote(
            stage.at[h], xs.at[row, source_col, :, source], send2.at[c, h], recv2.at[source_col, source], (h, row, c))

    def fill(h):
        before, after = lax.rem(h + NL - 1, NL), lax.rem(h + 1, NL)
        for q in range(12):
            stage[h, q] = buf[inside(tin[h, q])]
        for a in range(2):
            for j in range(2):
                stage[h, 12 + a * 2 + j] = buf[inside(tin[before, a * 6 + 2 + j])]
                stage[h, 16 + a * 2 + j] = buf[inside(tin[after, a * 6 + 2 + j])]

    @pl.loop(1, NL)
    def _(k):
        h = lax.rem(me + k, NL)
        fill(h)
        deliver(h, col, me, col).start()
        deliver(h, 1 - col, me, col).start()

    fill(me)
    deliver(me, 1 - col, me, col).start()
    here2 = pltpu.make_async_copy(stage.at[me], xs.at[row, col, :, me], local.at[3])
    here2.start()

    def swap(p, r):
        return remote(xs.at[r, :, :, p], xs.at[r, :, :, p], swap_send.at[p], swap_recv.at[p], (me, 1 - row, col))

    @pl.loop(1, NL)
    def _(k):
        p = lax.rem(me + NL - k, NL)
        deliver(me, col, p, 0).wait_recv()
        deliver(me, col, p, 1).wait_recv()
        swap(p, row).start()

    deliver(me, col, me, 1 - col).wait_recv()
    here2.wait()
    swap(me, row).start()

    @pl.loop(0, NL)
    def _(p):
        swap(p, 1 - row).wait_recv()

    multiply(me, row, col, xs, hi, lo, y)

    def result(p, r, source, member):
        return remote(y.at[r, :, p], srt.at[pl.ds(source * 12 + member * 6, 6)], send3.at[r, p], recv3.at[source, member], (p, r, col))

    @pl.loop(1, NL)
    def _(k):
        p = lax.rem(me + k, NL)
        result(p, row, me, row).start()
        result(p, 1 - row, me, row).start()

    result(me, 1 - row, me, row).start()
    here3 = pltpu.make_async_copy(y.at[row, :, me], srt.at[pl.ds(me * 12 + row * 6, 6)], local.at[4])
    here3.start()

    @pl.loop(1, NL)
    def _(k):
        h = lax.rem(me + NL - k, NL)
        result(me, row, h, 0).wait_recv()
        result(me, row, h, 1).wait_recv()

    result(me, row, me, 1 - row).wait_recv()
    here3.wait()

    def home(p, owner):
        return remote(stage2.at[p], out_ref.at[:, owner], send4.at[p], recv4.at[owner], (p, row, col))

    def fill_home(p):
        for jj in range(2):
            for s in range(6):
                stage2[p, jj * 6 + s] = srt[inside(tout[jj * 32 + p, s])]

    @pl.loop(1, NL)
    def _(k):
        p = lax.rem(me + k, NL)
        fill_home(p)
        home(p, me).start()

    fill_home(me)
    here4 = pltpu.make_async_copy(stage2.at[me], out_ref.at[:, me], local.at[5])
    here4.start()
    others(lambda p: home(p, p).wait_recv())
    here4.wait()

    @pl.loop(1, NL)
    def _(k):
        p = lax.rem(me + k, NL)
        pattern_copy(p, me).wait_send()
        spread(p, me).wait_send()
        deliver(p, col, me, col).wait_send()
        deliver(p, 1 - col, me, col).wait_send()
        swap(p, row).wait_send()
        result(p, 0, me, row).wait_send()
        result(p, 1, me, row).wait_send()
        home(p, me).wait_send()

    deliver(me, 1 - col, me, col).wait_send()
    swap(me, row).wait_send()
    result(me, 1 - row, me, row).wait_send()


ANY = pl.BlockSpec(memory_space=pl.ANY)
VMEM = pl.BlockSpec(memory_space=pltpu.VMEM)


def body(x_blocks, block_cols):
    f32, bf16, i32 = jnp.float32, jnp.bfloat16, jnp.int32
    vmem, smem, dma = pltpu.VMEM, pltpu.SMEM, pltpu.SemaphoreType.DMA
    out = pl.pallas_call(
        kernel,
        out_shape=jax.ShapeDtypeStruct((12, NL, ROWS, BLK), f32),
        in_specs=[VMEM, ANY],
        out_specs=ANY,
        scratch_shapes=[
            vmem((1, 128), i32), vmem((NL, 1, 128), i32), vmem((NL, 1, 128), i32),
            vmem((32, 128), i32), vmem((64, 128), i32), smem((32, 128), i32), smem((64, 128), i32),
            vmem((NL * 12, ROWS, BLK), f32), vmem((NL, 20, ROWS, BLK), f32), vmem((2, 2, 20, NL, ROWS, BLK), f32),
            vmem((5, 512, 512), bf16), vmem((5, 512, 512), bf16),
            vmem((2, 6, NL, ROWS, BLK), f32), vmem((NL * 12, ROWS, BLK), f32), vmem((NL, 12, ROWS, BLK), f32),
            dma((NL,)), dma((NL,)), dma((NL,)), dma((NL,)), dma((2, NL)), dma((2, NL)), dma((NL,)), dma((NL,)),
            dma((2, NL)), dma((NL, 2)), dma((NL,)), dma((NL,)), dma((2,)), dma((6,)),
        ],
        compiler_params=pltpu.CompilerParams(
            collective_id=0, has_side_effects=True, vmem_limit_bytes=VMEM_LIMIT),
        name="step",
    )(block_cols, x_blocks.reshape(12, NL, ROWS, BLK))
    return out.reshape(x_blocks.shape)


def solution(mesh):
    return jax.shard_map(
        body,
        mesh=mesh,
        in_specs=(P("row", "layer", "col", None, None, None), P("row", "layer", "col", None)),
        out_specs=P("row", "layer", "col", None, None, None),
        check_vma=False,
    )
```

```python
import functools

import jax
import jax.numpy as jnp
from jax import lax
from jax.experimental import pallas as pl
from jax.experimental.pallas import tpu as pltpu
from jax.sharding import PartitionSpec as P

MESH = pl.DeviceIdType.MESH
NL = 32
ROWS = 4
BLK = 128
MAIN = 17
SIDE = 14
VMEM_LIMIT = 56 * 1024 * 1024


def my_ids():
    return lax.axis_index("layer"), lax.axis_index("row"), lax.axis_index("col")


def dot_nt(a, b):
    return lax.dot_general(a, b, (((1,), (1,)), ((), ())), preferred_element_type=jnp.float32)


def dot_nn(a, b):
    return jnp.dot(a, b, preferred_element_type=jnp.float32)


def roll_groups(a, shift):
    return jnp.concatenate([a[shift:], a[:shift]], axis=0)


def order_tables(row, own, other):
    f32, bf16 = jnp.float32, jnp.bfloat16
    is_first = row == 0
    own = own.astype(f32)
    other = other.astype(f32)
    pat0 = jnp.where(is_first, own, other)
    pat1 = jnp.where(is_first, other, own)

    def rows_of(pat):
        return jnp.concatenate([pat[:, 0:6], pat[:, 6:12]], axis=0)

    def member(pat):
        iota = lax.broadcasted_iota(jnp.int32, (64, 64), 1).astype(f32)
        total = jnp.zeros((64, 64), f32)
        for s in range(6):
            total = total + jnp.where(pat[:, s:s + 1] == iota, 1.0, 0.0)
        return total

    def mask(cond):
        return jnp.where(cond, 1.0, 0.0)

    p0, p1 = rows_of(pat0), rows_of(pat1)
    m0, m1 = member(p0), member(p1)
    m0b, m1b = m0.astype(bf16), m1.astype(bf16)
    common = dot_nt(m0b, m0b)
    reach2 = mask(common > 1.0)
    b2 = reach2.astype(bf16)
    reach4 = mask(dot_nn(b2, b2) > 0.5)
    b4 = reach4.astype(bf16)
    b8 = mask(dot_nn(b4, b4) > 0.5).astype(bf16)
    lane = lax.broadcasted_iota(jnp.int32, (1, 64), 1).astype(f32)
    sub = lax.broadcasted_iota(jnp.int32, (64, 64), 0).astype(f32)
    first = common[0:1, :]
    start = jnp.min(jnp.where(first == 4.0, lane, 1000.0), axis=1, keepdims=True)
    second = jnp.sum(jnp.where(sub == start, common, 0.0), axis=0, keepdims=True)
    t = jnp.concatenate([mask(first > 5.0), mask(first > 3.0), mask(second > 5.0), mask(second > 3.0)], axis=0)
    for b in (b2, b4, b8):
        t = jnp.concatenate([t, mask(dot_nn(t.astype(bf16), b) > 0.5)], axis=0)
    which = lax.broadcasted_iota(jnp.int32, (32, 64), 0)
    from_first = jnp.bitwise_and(which, 3) < 2
    dist0 = 16.0 - jnp.sum(jnp.where(from_first, t, 0.0), axis=0, keepdims=True)
    dist1 = 16.0 - jnp.sum(jnp.where(from_first, 0.0, t), axis=0, keepdims=True)
    pos0 = jnp.where(dist1 < dist0, dist0, jnp.where(dist0 == 0.0, 0.0, 32.0 - dist0))
    group = lax.broadcasted_iota(jnp.int32, (32, 64), 0).astype(f32)
    g0 = mask(group == pos0)

    def centre(c):
        return mask(roll_groups(c, -1) + c + roll_groups(c, 1) > 5.0)

    hc = centre(dot_nn(g0.astype(bf16), m0b))
    g1 = centre(dot_nt(hc.astype(bf16), m1b))
    gr = jnp.where(is_first, g0, g1)
    pr = jnp.where(is_first, p0, p1)

    lanes = lax.broadcasted_iota(jnp.int32, (32, 64), 1)
    natural = (jnp.bitwise_and(lanes, 31) * 2 + jnp.right_shift(lanes, 5)).astype(f32)
    column = lanes.astype(f32)
    row_lo = jnp.min(jnp.where(gr > 0.5, natural, 1000.0), axis=1, keepdims=True)
    row_hi = jnp.max(jnp.where(gr > 0.5, natural, -1.0), axis=1, keepdims=True)
    col_lo = jnp.min(jnp.where(hc > 0.5, column, 1000.0), axis=1, keepdims=True)
    col_hi = jnp.max(jnp.where(hc > 0.5, column, -1.0), axis=1, keepdims=True)

    prb = jnp.concatenate([pr, jnp.zeros((64, 122), f32)], axis=1).astype(bf16)
    out_lane = lax.broadcasted_iota(jnp.int32, (32, 128), 1)
    slot_iota = out_lane.astype(f32)
    table = jnp.zeros((32, 128), f32)
    for a, members in enumerate((row_lo, row_hi)):
        chosen = mask((gr > 0.5) & (natural == members))
        cols = dot_nn(chosen.astype(bf16), prb)
        cols = jnp.where(out_lane < 6, cols, -1.0)
        for d in range(3):
            for j, cmem in enumerate((col_lo, col_hi)):
                target = roll_groups(cmem, d - 1) if d != 1 else cmem
                slot = jnp.sum(jnp.where(cols == target, slot_iota, 0.0), axis=1, keepdims=True)
                table = jnp.where(out_lane == a * 6 + d * 2 + j, members * 6.0 + slot, table)
    tin = jnp.clip(table, 0.0, 383.0).astype(jnp.int32)

    eye = mask(lax.broadcasted_iota(jnp.int32, (64, 64), 0) == lax.broadcasted_iota(jnp.int32, (64, 64), 1)).astype(bf16)
    extra = lax.broadcasted_iota(jnp.int32, (32, 64), 0).astype(f32)
    grt = dot_nt(eye, gr.astype(bf16))
    gi = jnp.sum(grt * lax.broadcasted_iota(jnp.int32, (64, 32), 1).astype(f32), axis=1, keepdims=True)
    hi_flag = mask((gr > 0.5) & (natural == row_hi))
    ai = jnp.sum(dot_nt(eye, hi_flag.astype(bf16)), axis=1, keepdims=True)
    gcol = jnp.sum(hc * extra, axis=0, keepdims=True)
    jcol = jnp.sum(mask((hc > 0.5) & (column == col_hi)), axis=0, keepdims=True)
    code = gcol * 2.0 + jcol
    iota64 = lax.broadcasted_iota(jnp.int32, (64, 64), 1).astype(f32)
    lane64 = lax.broadcasted_iota(jnp.int32, (64, 128), 1)
    out = jnp.zeros((64, 128), jnp.int32)
    gi_i, ai_i = gi.astype(jnp.int32), ai.astype(jnp.int32)
    for s in range(6):
        val = jnp.sum(jnp.where(pr[:, s:s + 1] == iota64, code, 0.0), axis=1, keepdims=True).astype(jnp.int32)
        gc, jc = jnp.right_shift(val, 1), jnp.bitwise_and(val, 1)
        d = jnp.bitwise_and(gi_i - gc + 1, 31)
        out = jnp.where(lane64 == s, gc * 12 + jc * 6 + d * 2 + ai_i, out)
    return tin, jnp.clip(out, 0, 383)


def inside(place):
    return jnp.minimum(jnp.maximum(place, 0), NL * 12 - 1)


def split(value):
    high = value.astype(jnp.bfloat16)
    return high, (value - high.astype(jnp.float32)).astype(jnp.bfloat16)


def multiply(row, col, xs, hi, lo, y, send_half):
    def put(part, r, a, c, j, block):
        rows = pl.ds(pl.multiple_of(r * 256 + a * 128, 128), 128)
        cols = pl.ds(pl.multiple_of(c * 256 + j * 128, 128), 128)
        high, low = split(block)
        hi[part, rows, cols] = high
        lo[part, rows, cols] = low

    def piece(r, n):
        return xs[r, n].reshape(BLK, BLK)

    @pl.loop(0, 16)
    def _(n):
        r, c, a, j = n // 8, lax.rem(n // 4, 2), lax.rem(n // 2, 2), lax.rem(n, 2)
        base = MAIN * lax.rem(r + c, 2) + a * 2 + j
        put(3, r, a, c, j, piece(r, base))
        put(4, r, a, c, j, piece(r, base + 4))

    @pl.loop(0, 3)
    def _(part):
        for r in range(2):
            put(part, r, 0, r, 0, piece(r, 8 + part * 2))
            mixed = piece(r, 9 + part * 2)
            put(part, r, 0, r, 1, mixed)
            put(part, r, 1, r, 0, mixed.T)
            put(part, r, 1, r, 1, piece(r, 14 + part))
            for e, (at, aj) in enumerate((((0, 0), (0, 1)), ((0, 1), (1, 1)))[r]):
                block = piece(r, MAIN + 8 + part * 2 + e)
                put(part, r, at, 1 - r, aj, block)
                put(part, 1 - r, aj, r, at, block.T)

    def mul(pairs, half=None):
        total = None
        for (stacked, high), part, transposed in pairs:
            if half is None:
                bh, bl = hi[part], lo[part]
            elif transposed:
                bh, bl = hi[part, half, :], lo[part, half, :]
            else:
                bh, bl = hi[part, :, half], lo[part, :, half]
            dot = dot_nt if transposed else dot_nn
            both = dot(stacked, bh)
            term = both[:BLK] + both[BLK:] + dot(high, bl)
            total = term if total is None else total + term
        return total

    def apply(w, half=None):
        left, mid, right = w
        return (
            mul([(left, 0, False), (mid, 3, False)], half),
            mul([(left, 3, True), (mid, 1, False), (right, 4, True)], half),
            mul([(mid, 4, False), (right, 2, False)], half),
        )

    def stack(high, low):
        return jnp.concatenate([high, low], axis=0), high

    offset = col * 256 + row * 128
    mine = pl.ds(pl.multiple_of(offset, 128), 128)
    left, mid, right = apply([stack(hi[part, mine, :], lo[part, mine, :]) for part in (3, 1, 4)])
    q = lax.broadcasted_iota(jnp.int32, (BLK, 512), 0)
    k = lax.broadcasted_iota(jnp.int32, (BLK, 512), 1)
    mid = jnp.where(k == q + offset, 3.0, 0.0) - mid
    s = [stack(*split(-left)), stack(*split(mid)), stack(*split(-right))]
    for r in range(2):
        for d, part in enumerate(apply(s, slice(r * 256, r * 256 + 256))):
            half = 0.5 * part
            for a in range(2):
                y[r, d * 2 + a] = half[:, a * 128:a * 128 + 128].T.reshape(NL, ROWS, BLK)
        send_half(r)


def kernel(
    cols_ref, x_ref, out_ref, pat, own, other, tin_v, tout_v, tin, tout, buf, stage, xs, hi, lo, y, srt, stage2,
    psend, precv, send1, recv1, send2, recv2, swap_send, swap_recv, send3, recv3, send4, recv4, core, local,
):
    me, row, col = my_ids()
    barrier = pltpu.get_barrier_semaphore()

    def signal(device):
        pl.semaphore_signal(barrier, inc=1, device_id=device, device_id_type=MESH)

    signal((me, 1 - row, col))
    signal((me, row, 1 - col))

    @pl.loop(1, NL)
    def _(k):
        signal((lax.rem(me + k, NL), row, col))

    for jj in range(2):
        pat[0:1, jj * 6:jj * 6 + 6] = cols_ref[0, jj]
    pl.semaphore_wait(barrier, NL + 1)

    def remote(src, dst, send, recv, device):
        return pltpu.make_async_remote_copy(src, dst, send, recv, device_id=device, device_id_type=MESH)

    def others(step):
        @pl.loop(1, NL)
        def _(k):
            step(lax.rem(me + k, NL))

    def wait_bytes(ref, sem):
        pltpu.make_async_copy(ref, ref, sem).wait()

    def pattern_copy(p):
        return remote(pat, own.at[me], psend, precv, (p, row, col))

    def spread(p):
        return remote(x_ref.at[:, p], buf.at[pl.ds(me * 12, 12)], send1, recv1, (p, row, col))

    others(lambda p: pattern_copy(p).start())
    others(lambda p: spread(p).start())
    here1 = pltpu.make_async_copy(x_ref.at[:, me], buf.at[pl.ds(me * 12, 12)], local.at[0])
    here1.start()
    own[me] = pat[...]
    wait_bytes(own.at[pl.ds(0, NL - 1)], precv)
    swap_pattern = remote(own, other, core.at[0], core.at[1], (me, 1 - row, col))
    swap_pattern.start()
    swap_pattern.wait()
    tin_v[...], tout_v[...] = order_tables(row, own[...].reshape(NL, 128), other[...].reshape(NL, 128))
    moves = [
        pltpu.make_async_copy(vector, scalar, local.at[1 + n])
        for n, (vector, scalar) in enumerate(((tin_v, tin), (tout_v, tout)))
    ]
    for move in moves:
        move.start()
    for move in moves:
        move.wait()
    here1.wait()
    wait_bytes(buf.at[pl.ds(0, (NL - 1) * 12)], recv1)

    def deliver(h, c, source, same):
        base, count = (0, MAIN) if same else (MAIN, SIDE)
        return remote(
            stage.at[h, pl.ds(0, count)], xs.at[row, pl.ds(base, count), source],
            send2.at[c, h], recv2.at[1 - int(same), source], (h, row, c))

    lower = row * (1 - col)

    def fill(h):
        for a in range(2):
            for j in range(2):
                stage[h, a * 2 + j] = buf[inside(tin[h, a * 6 + j])]
                stage[h, 4 + a * 2 + j] = buf[inside(tin[h, a * 6 + 4 + j])]
        for n, g in enumerate((lax.rem(h + NL - 1, NL), h, lax.rem(h + 1, NL))):
            stage[h, 8 + n * 2] = buf[inside(tin[g, 2 + lower])]
            stage[h, 9 + n * 2] = buf[inside(tin[g, 3 + 6 * lower])]
            stage[h, 14 + n] = buf[inside(tin[g, 9])]

    def by_class(step):
        for same in (True, False):
            pl.when((row == col) if same else (row != col))(functools.partial(step, same))

    def send_pieces(same):
        @pl.loop(1, NL)
        def _(k):
            h = lax.rem(me + k, NL)
            fill(h)
            deliver(h, col, me, same).start()
            deliver(h, 1 - col, me, same).start()

        fill(me)
        deliver(me, 1 - col, me, same).start()
        base, count = (0, MAIN) if same else (MAIN, SIDE)
        here = pltpu.make_async_copy(stage.at[me, pl.ds(0, count)], xs.at[row, pl.ds(base, count), me], local.at[3])
        here.start()
        here.wait()

    by_class(send_pieces)
    wait_bytes(own.at[pl.ds(0, NL - 1)], psend)
    wait_bytes(buf.at[pl.ds(0, (NL - 1) * 12)], send1)

    def swap(p, r):
        return remote(xs.at[r, :, p], xs.at[r, :, p], swap_send, swap_recv, (me, 1 - row, col))

    @pl.loop(1, NL)
    def _(k):
        p = lax.rem(me + NL - k, NL)
        deliver(me, col, p, True).wait_recv()
        deliver(me, col, p, False).wait_recv()
        swap(p, row).start()

    by_class(lambda same: deliver(me, col, me, not same).wait_recv())
    swap(me, row).start()
    wait_bytes(xs.at[1 - row], swap_recv)

    def result(p, r):
        return remote(y.at[r, :, p], srt.at[pl.ds(me * 12 + row * 6, 6)], send3, recv3, (p, r, col))

    here3 = pltpu.make_async_copy(y.at[row, :, me], srt.at[pl.ds(me * 12 + row * 6, 6)], local.at[4])

    def send_half(r):
        @pl.loop(1, NL)
        def _(k):
            result(lax.rem(me + k, NL), r).start()

        @pl.when(r == row)
        def _():
            here3.start()

        @pl.when(r != row)
        def _():
            result(me, r).start()

    multiply(row, col, xs, hi, lo, y, send_half)

    def sent_pieces(same):
        others(lambda p: deliver(p, col, me, same).wait_send())
        others(lambda p: deliver(p, 1 - col, me, same).wait_send())
        deliver(me, 1 - col, me, same).wait_send()

    by_class(sent_pieces)
    wait_bytes(xs.at[row], swap_send)
    here3.wait()
    wait_bytes(srt.at[pl.ds(0, (2 * NL - 1) * 6)], recv3)

    def home(p):
        return remote(stage2.at[p], out_ref.at[:, me], send4, recv4, (p, row, col))

    def fill_home(p):
        for jj in range(2):
            for s in range(6):
                stage2[p, jj * 6 + s] = srt[inside(tout[jj * 32 + p, s])]

    @pl.loop(1, NL)
    def _(k):
        p = lax.rem(me + k, NL)
        fill_home(p)
        home(p).start()

    fill_home(me)
    here4 = pltpu.make_async_copy(stage2.at[me], out_ref.at[:, me], local.at[5])
    here4.start()
    wait_bytes(srt.at[pl.ds(0, (2 * NL - 1) * 6)], send3)
    wait_bytes(stage2.at[pl.ds(0, NL - 1)], send4)
    here4.wait()
    wait_bytes(stage2.at[pl.ds(0, NL - 1)], recv4)


ANY = pl.BlockSpec(memory_space=pl.ANY)
VMEM = pl.BlockSpec(memory_space=pltpu.VMEM)


def body(x_blocks, block_cols):
    f32, bf16, i32 = jnp.float32, jnp.bfloat16, jnp.int32
    vmem, smem, dma = pltpu.VMEM, pltpu.SMEM, pltpu.SemaphoreType.DMA
    out = pl.pallas_call(
        kernel,
        out_shape=jax.ShapeDtypeStruct((12, NL, ROWS, BLK), f32),
        in_specs=[VMEM, ANY],
        out_specs=ANY,
        scratch_shapes=[
            vmem((1, 128), i32), vmem((NL, 1, 128), i32), vmem((NL, 1, 128), i32),
            vmem((32, 128), i32), vmem((64, 128), i32), smem((32, 128), i32), smem((64, 128), i32),
            vmem((NL * 12, ROWS, BLK), f32), vmem((NL, MAIN, ROWS, BLK), f32), vmem((2, MAIN + SIDE, NL, ROWS, BLK), f32),
            vmem((5, 512, 512), bf16), vmem((5, 512, 512), bf16),
            vmem((2, 6, NL, ROWS, BLK), f32), vmem((NL * 12, ROWS, BLK), f32), vmem((NL, 12, ROWS, BLK), f32),
            dma, dma, dma, dma, dma((2, NL)), dma((2, NL)), dma, dma,
            dma, dma, dma, dma, dma((2,)), dma((6,)),
        ],
        compiler_params=pltpu.CompilerParams(
            collective_id=0, has_side_effects=True, vmem_limit_bytes=VMEM_LIMIT),
        name="step",
    )(block_cols, x_blocks.reshape(12, NL, ROWS, BLK))
    return out.reshape(x_blocks.shape)


def solution(mesh):
    return jax.shard_map(
        body,
        mesh=mesh,
        in_specs=(P("row", "layer", "col", None, None, None), P("row", "layer", "col", None)),
        out_specs=P("row", "layer", "col", None, None, None),
        check_vma=False,
    )
```

```python
import functools

import jax
import jax.numpy as jnp
from jax import lax
from jax.experimental import pallas as pl
from jax.experimental.pallas import tpu as pltpu
from jax.sharding import PartitionSpec as P

MESH = pl.DeviceIdType.MESH
NL = 32
ROWS = 4
BLK = 128
MAIN = 17
SIDE = 14
STRIDE = 3
VMEM_LIMIT = 56 * 1024 * 1024


def my_ids():
    return lax.axis_index("layer"), lax.axis_index("row"), lax.axis_index("col")


def dot_nt(a, b):
    return lax.dot_general(a, b, (((1,), (1,)), ((), ())), preferred_element_type=jnp.float32)


def dot_nn(a, b):
    return jnp.dot(a, b, preferred_element_type=jnp.float32)


def roll_groups(a, shift):
    return jnp.concatenate([a[shift:], a[:shift]], axis=0)


def order_tables(row, own, other):
    f32, bf16 = jnp.float32, jnp.bfloat16
    is_first = row == 0
    own = own.astype(f32)
    other = other.astype(f32)
    pat0 = jnp.where(is_first, own, other)
    pat1 = jnp.where(is_first, other, own)

    def rows_of(pat):
        return jnp.concatenate([pat[:, 0:6], pat[:, 6:12]], axis=0)

    def member(pat):
        iota = lax.broadcasted_iota(jnp.int32, (64, 64), 1).astype(f32)
        total = jnp.zeros((64, 64), f32)
        for s in range(6):
            total = total + jnp.where(pat[:, s:s + 1] == iota, 1.0, 0.0)
        return total

    def mask(cond):
        return jnp.where(cond, 1.0, 0.0)

    p0, p1 = rows_of(pat0), rows_of(pat1)
    m0, m1 = member(p0), member(p1)
    m0b, m1b = m0.astype(bf16), m1.astype(bf16)
    common = dot_nt(m0b, m0b)
    reach2 = mask(common > 1.0)
    b2 = reach2.astype(bf16)
    reach4 = mask(dot_nn(b2, b2) > 0.5)
    b4 = reach4.astype(bf16)
    b8 = mask(dot_nn(b4, b4) > 0.5).astype(bf16)
    lane = lax.broadcasted_iota(jnp.int32, (1, 64), 1).astype(f32)
    sub = lax.broadcasted_iota(jnp.int32, (64, 64), 0).astype(f32)
    first = common[0:1, :]
    start = jnp.min(jnp.where(first == 4.0, lane, 1000.0), axis=1, keepdims=True)
    second = jnp.sum(jnp.where(sub == start, common, 0.0), axis=0, keepdims=True)
    t = jnp.concatenate([mask(first > 5.0), mask(first > 3.0), mask(second > 5.0), mask(second > 3.0)], axis=0)
    for b in (b2, b4, b8):
        t = jnp.concatenate([t, mask(dot_nn(t.astype(bf16), b) > 0.5)], axis=0)
    which = lax.broadcasted_iota(jnp.int32, (32, 64), 0)
    from_first = jnp.bitwise_and(which, 3) < 2
    dist0 = 16.0 - jnp.sum(jnp.where(from_first, t, 0.0), axis=0, keepdims=True)
    dist1 = 16.0 - jnp.sum(jnp.where(from_first, 0.0, t), axis=0, keepdims=True)
    pos0 = jnp.where(dist1 < dist0, dist0, jnp.where(dist0 == 0.0, 0.0, 32.0 - dist0))
    group = lax.broadcasted_iota(jnp.int32, (32, 64), 0).astype(f32)
    g0 = mask(group == pos0)

    def centre(c):
        return mask(roll_groups(c, -1) + c + roll_groups(c, 1) > 5.0)

    hc = centre(dot_nn(g0.astype(bf16), m0b))
    g1 = centre(dot_nt(hc.astype(bf16), m1b))
    gr = jnp.where(is_first, g0, g1)
    pr = jnp.where(is_first, p0, p1)

    lanes = lax.broadcasted_iota(jnp.int32, (32, 64), 1)
    natural = (jnp.bitwise_and(lanes, 31) * 2 + jnp.right_shift(lanes, 5)).astype(f32)
    column = lanes.astype(f32)
    row_lo = jnp.min(jnp.where(gr > 0.5, natural, 1000.0), axis=1, keepdims=True)
    row_hi = jnp.max(jnp.where(gr > 0.5, natural, -1.0), axis=1, keepdims=True)
    col_lo = jnp.min(jnp.where(hc > 0.5, column, 1000.0), axis=1, keepdims=True)
    col_hi = jnp.max(jnp.where(hc > 0.5, column, -1.0), axis=1, keepdims=True)

    prb = jnp.concatenate([pr, jnp.zeros((64, 122), f32)], axis=1).astype(bf16)
    out_lane = lax.broadcasted_iota(jnp.int32, (32, 128), 1)
    slot_iota = out_lane.astype(f32)
    table = jnp.zeros((32, 128), f32)
    for a, members in enumerate((row_lo, row_hi)):
        chosen = mask((gr > 0.5) & (natural == members))
        cols = dot_nn(chosen.astype(bf16), prb)
        cols = jnp.where(out_lane < 6, cols, -1.0)
        for d in range(3):
            for j, cmem in enumerate((col_lo, col_hi)):
                target = roll_groups(cmem, d - 1) if d != 1 else cmem
                slot = jnp.sum(jnp.where(cols == target, slot_iota, 0.0), axis=1, keepdims=True)
                table = jnp.where(out_lane == a * 6 + d * 2 + j, members * 6.0 + slot, table)
    tin = jnp.clip(table, 0.0, 383.0).astype(jnp.int32)

    eye = mask(lax.broadcasted_iota(jnp.int32, (64, 64), 0) == lax.broadcasted_iota(jnp.int32, (64, 64), 1)).astype(bf16)
    extra = lax.broadcasted_iota(jnp.int32, (32, 64), 0).astype(f32)
    grt = dot_nt(eye, gr.astype(bf16))
    gi = jnp.sum(grt * lax.broadcasted_iota(jnp.int32, (64, 32), 1).astype(f32), axis=1, keepdims=True)
    hi_flag = mask((gr > 0.5) & (natural == row_hi))
    ai = jnp.sum(dot_nt(eye, hi_flag.astype(bf16)), axis=1, keepdims=True)
    gcol = jnp.sum(hc * extra, axis=0, keepdims=True)
    jcol = jnp.sum(mask((hc > 0.5) & (column == col_hi)), axis=0, keepdims=True)
    code = gcol * 2.0 + jcol
    iota64 = lax.broadcasted_iota(jnp.int32, (64, 64), 1).astype(f32)
    lane64 = lax.broadcasted_iota(jnp.int32, (64, 128), 1)
    out = jnp.zeros((64, 128), jnp.int32)
    gi_i, ai_i = gi.astype(jnp.int32), ai.astype(jnp.int32)
    for s in range(6):
        val = jnp.sum(jnp.where(pr[:, s:s + 1] == iota64, code, 0.0), axis=1, keepdims=True).astype(jnp.int32)
        gc, jc = jnp.right_shift(val, 1), jnp.bitwise_and(val, 1)
        d = jnp.bitwise_and(gi_i - gc + 1, 31)
        out = jnp.where(lane64 == s, gc * 12 + jc * 6 + d * 2 + ai_i, out)
    return tin, jnp.clip(out, 0, 383)


def inside(place):
    return jnp.minimum(jnp.maximum(place, 0), NL * 12 - 1)


def split(value):
    high = value.astype(jnp.bfloat16)
    return high, (value - high.astype(jnp.float32)).astype(jnp.bfloat16)


def multiply(row, col, xs, hi, lo, y, send_half):
    def put(part, r, a, c, j, block):
        rows = pl.ds(pl.multiple_of(r * 256 + a * 128, 128), 128)
        cols = pl.ds(pl.multiple_of(c * 256 + j * 128, 128), 128)
        high, low = split(block)
        hi[part, rows, cols] = high
        lo[part, rows, cols] = low

    def piece(r, n):
        return xs[r, n].reshape(BLK, BLK)

    @pl.loop(0, 16)
    def _(n):
        r, c, a, j = n // 8, lax.rem(n // 4, 2), lax.rem(n // 2, 2), lax.rem(n, 2)
        base = MAIN * lax.rem(r + c, 2) + a * 2 + j
        put(3, r, a, c, j, piece(r, base))
        put(4, r, a, c, j, piece(r, base + 4))

    @pl.loop(0, 3)
    def _(part):
        for r in range(2):
            put(part, r, 0, r, 0, piece(r, 8 + part * 2))
            mixed = piece(r, 9 + part * 2)
            put(part, r, 0, r, 1, mixed)
            put(part, r, 1, r, 0, mixed.T)
            put(part, r, 1, r, 1, piece(r, 14 + part))
            for e, (at, aj) in enumerate((((0, 0), (0, 1)), ((0, 1), (1, 1)))[r]):
                block = piece(r, MAIN + 8 + part * 2 + e)
                put(part, r, at, 1 - r, aj, block)
                put(part, 1 - r, aj, r, at, block.T)

    def mul(pairs, half=None):
        total = None
        for (stacked, high), part, transposed in pairs:
            if half is None:
                bh, bl = hi[part], lo[part]
            elif transposed:
                bh, bl = hi[part, half, :], lo[part, half, :]
            else:
                bh, bl = hi[part, :, half], lo[part, :, half]
            dot = dot_nt if transposed else dot_nn
            both = dot(stacked, bh)
            term = both[:BLK] + both[BLK:] + dot(high, bl)
            total = term if total is None else total + term
        return total

    def apply(w, half=None):
        left, mid, right = w
        return (
            mul([(left, 0, False), (mid, 3, False)], half),
            mul([(left, 3, True), (mid, 1, False), (right, 4, True)], half),
            mul([(mid, 4, False), (right, 2, False)], half),
        )

    def stack(high, low):
        return jnp.concatenate([high, low], axis=0), high

    offset = col * 256 + row * 128
    mine = pl.ds(pl.multiple_of(offset, 128), 128)
    left, mid, right = apply([stack(hi[part, mine, :], lo[part, mine, :]) for part in (3, 1, 4)])
    q = lax.broadcasted_iota(jnp.int32, (BLK, 512), 0)
    k = lax.broadcasted_iota(jnp.int32, (BLK, 512), 1)
    mid = jnp.where(k == q + offset, 3.0, 0.0) - mid
    s = [stack(*split(-left)), stack(*split(mid)), stack(*split(-right))]
    for r in range(2):
        for d, part in enumerate(apply(s, slice(r * 256, r * 256 + 256))):
            half = 0.5 * part
            for a in range(2):
                y[r, d * 2 + a] = half[:, a * 128:a * 128 + 128].T.reshape(NL, ROWS, BLK)
        send_half(r)


def kernel(
    cols_ref, x_ref, out_ref, pat, own, other, tin_v, tout_v, tin, tout, buf, stage, xs, hi, lo, y, srt, stage2,
    psend, precv, send1, recv1, send2, recv2, swap_send, swap_recv, send3, recv3, send4, recv4, core, local,
):
    me, row, col = my_ids()
    barrier = pltpu.get_barrier_semaphore()

    def signal(device):
        pl.semaphore_signal(barrier, inc=1, device_id=device, device_id_type=MESH)

    signal((me, 1 - row, col))
    signal((me, row, 1 - col))

    @pl.loop(1, NL)
    def _(k):
        signal((lax.rem(me + k, NL), row, col))

    for jj in range(2):
        pat[0:1, jj * 6:jj * 6 + 6] = cols_ref[0, jj]
    pl.semaphore_wait(barrier, NL + 1)

    def remote(src, dst, send, recv, device):
        return pltpu.make_async_remote_copy(src, dst, send, recv, device_id=device, device_id_type=MESH)

    def others(step):
        @pl.loop(1, NL)
        def _(k):
            step(lax.rem(me + k, NL))

    def start_others(step):
        @pl.loop(0, NL)
        def _(k):
            p = lax.rem(STRIDE * k + me, NL)
            pl.when(p != me)(lambda: step(p))

    def wait_bytes(ref, sem):
        pltpu.make_async_copy(ref, ref, sem).wait()

    def pattern_copy(p):
        return remote(pat, own.at[me], psend, precv, (p, row, col))

    def spread(p):
        return remote(x_ref.at[:, p], buf.at[pl.ds(me * 12, 12)], send1, recv1, (p, row, col))

    start_others(lambda p: pattern_copy(p).start())
    start_others(lambda p: spread(p).start())
    here1 = pltpu.make_async_copy(x_ref.at[:, me], buf.at[pl.ds(me * 12, 12)], local.at[0])
    here1.start()
    own[me] = pat[...]
    wait_bytes(own.at[pl.ds(0, NL - 1)], precv)
    swap_pattern = remote(own, other, core.at[0], core.at[1], (me, 1 - row, col))
    swap_pattern.start()
    swap_pattern.wait()
    tin_v[...], tout_v[...] = order_tables(row, own[...].reshape(NL, 128), other[...].reshape(NL, 128))
    moves = [
        pltpu.make_async_copy(vector, scalar, local.at[1 + n])
        for n, (vector, scalar) in enumerate(((tin_v, tin), (tout_v, tout)))
    ]
    for move in moves:
        move.start()
    for move in moves:
        move.wait()
    here1.wait()
    wait_bytes(buf.at[pl.ds(0, (NL - 1) * 12)], recv1)

    def deliver(h, c, source, same):
        base, count = (0, MAIN) if same else (MAIN, SIDE)
        return remote(
            stage.at[h, pl.ds(0, count)], xs.at[row, pl.ds(base, count), source],
            send2.at[c, h], recv2.at[1 - int(same), source], (h, row, c))

    lower = row * (1 - col)

    def fill(h):
        for a in range(2):
            for j in range(2):
                stage[h, a * 2 + j] = buf[inside(tin[h, a * 6 + j])]
                stage[h, 4 + a * 2 + j] = buf[inside(tin[h, a * 6 + 4 + j])]
        for n, g in enumerate((lax.rem(h + NL - 1, NL), h, lax.rem(h + 1, NL))):
            stage[h, 8 + n * 2] = buf[inside(tin[g, 2 + lower])]
            stage[h, 9 + n * 2] = buf[inside(tin[g, 3 + 6 * lower])]
            stage[h, 14 + n] = buf[inside(tin[g, 9])]

    def by_class(step):
        for same in (True, False):
            pl.when((row == col) if same else (row != col))(functools.partial(step, same))

    def send_pieces(same):
        def step(h):
            fill(h)
            deliver(h, col, me, same).start()
            deliver(h, 1 - col, me, same).start()

        start_others(step)
        fill(me)
        deliver(me, 1 - col, me, same).start()
        base, count = (0, MAIN) if same else (MAIN, SIDE)
        here = pltpu.make_async_copy(stage.at[me, pl.ds(0, count)], xs.at[row, pl.ds(base, count), me], local.at[3])
        here.start()
        here.wait()

    by_class(send_pieces)
    wait_bytes(own.at[pl.ds(0, NL - 1)], psend)
    wait_bytes(buf.at[pl.ds(0, (NL - 1) * 12)], send1)

    def swap(p, r):
        return remote(xs.at[r, :, p], xs.at[r, :, p], swap_send, swap_recv, (me, 1 - row, col))

    @pl.loop(1, NL)
    def _(k):
        p = lax.rem(me + NL - k, NL)
        deliver(me, col, p, True).wait_recv()
        deliver(me, col, p, False).wait_recv()
        swap(p, row).start()

    by_class(lambda same: deliver(me, col, me, not same).wait_recv())
    swap(me, row).start()
    wait_bytes(xs.at[1 - row], swap_recv)

    def result(p, r):
        return remote(y.at[r, :, p], srt.at[pl.ds(me * 12 + row * 6, 6)], send3, recv3, (p, r, col))

    here3 = pltpu.make_async_copy(y.at[row, :, me], srt.at[pl.ds(me * 12 + row * 6, 6)], local.at[4])

    def send_half(r):
        start_others(lambda p: result(p, r).start())

        @pl.when(r == row)
        def _():
            here3.start()

        @pl.when(r != row)
        def _():
            result(me, r).start()

    multiply(row, col, xs, hi, lo, y, send_half)

    def sent_pieces(same):
        others(lambda p: deliver(p, col, me, same).wait_send())
        others(lambda p: deliver(p, 1 - col, me, same).wait_send())
        deliver(me, 1 - col, me, same).wait_send()

    by_class(sent_pieces)
    wait_bytes(xs.at[row], swap_send)
    here3.wait()
    wait_bytes(srt.at[pl.ds(0, (2 * NL - 1) * 6)], recv3)

    def home(p):
        return remote(stage2.at[p], out_ref.at[:, me], send4, recv4, (p, row, col))

    def fill_home(p):
        for jj in range(2):
            for s in range(6):
                stage2[p, jj * 6 + s] = srt[inside(tout[jj * 32 + p, s])]

    def go_home(p):
        fill_home(p)
        home(p).start()

    start_others(go_home)
    fill_home(me)
    here4 = pltpu.make_async_copy(stage2.at[me], out_ref.at[:, me], local.at[5])
    here4.start()
    wait_bytes(srt.at[pl.ds(0, (2 * NL - 1) * 6)], send3)
    wait_bytes(stage2.at[pl.ds(0, NL - 1)], send4)
    here4.wait()
    wait_bytes(stage2.at[pl.ds(0, NL - 1)], recv4)


ANY = pl.BlockSpec(memory_space=pl.ANY)
VMEM = pl.BlockSpec(memory_space=pltpu.VMEM)


def body(x_blocks, block_cols):
    f32, bf16, i32 = jnp.float32, jnp.bfloat16, jnp.int32
    vmem, smem, dma = pltpu.VMEM, pltpu.SMEM, pltpu.SemaphoreType.DMA
    out = pl.pallas_call(
        kernel,
        out_shape=jax.ShapeDtypeStruct((12, NL, ROWS, BLK), f32),
        in_specs=[VMEM, ANY],
        out_specs=ANY,
        scratch_shapes=[
            vmem((1, 128), i32), vmem((NL, 1, 128), i32), vmem((NL, 1, 128), i32),
            vmem((32, 128), i32), vmem((64, 128), i32), smem((32, 128), i32), smem((64, 128), i32),
            vmem((NL * 12, ROWS, BLK), f32), vmem((NL, MAIN, ROWS, BLK), f32), vmem((2, MAIN + SIDE, NL, ROWS, BLK), f32),
            vmem((5, 512, 512), bf16), vmem((5, 512, 512), bf16),
            vmem((2, 6, NL, ROWS, BLK), f32), vmem((NL * 12, ROWS, BLK), f32), vmem((NL, 12, ROWS, BLK), f32),
            dma, dma, dma, dma, dma((2, NL)), dma((2, NL)), dma, dma,
            dma, dma, dma, dma, dma((2,)), dma((6,)),
        ],
        compiler_params=pltpu.CompilerParams(
            collective_id=0, has_side_effects=True, vmem_limit_bytes=VMEM_LIMIT),
        name="step",
    )(block_cols, x_blocks.reshape(12, NL, ROWS, BLK))
    return out.reshape(x_blocks.shape)


def solution(mesh):
    return jax.shard_map(
        body,
        mesh=mesh,
        in_specs=(P("row", "layer", "col", None, None, None), P("row", "layer", "col", None)),
        out_specs=P("row", "layer", "col", None, None, None),
        check_vma=False,
    )
```

```python
import functools

import jax
import jax.numpy as jnp
from jax import lax
from jax.experimental import pallas as pl
from jax.experimental.pallas import tpu as pltpu
from jax.sharding import PartitionSpec as P

MESH = pl.DeviceIdType.MESH
NL = 32
ROWS = 4
BLK = 128
MAIN = 17
SIDE = 14
STRIDE = 3
VMEM_LIMIT = 56 * 1024 * 1024


def my_ids():
    return lax.axis_index("layer"), lax.axis_index("row"), lax.axis_index("col")


def dot_nt(a, b):
    return lax.dot_general(a, b, (((1,), (1,)), ((), ())), preferred_element_type=jnp.float32)


def dot_nn(a, b):
    return jnp.dot(a, b, preferred_element_type=jnp.float32)


def roll_groups(a, shift):
    return jnp.concatenate([a[shift:], a[:shift]], axis=0)


def order_tables(row, own, other):
    f32, bf16 = jnp.float32, jnp.bfloat16
    is_first = row == 0
    own = own.astype(f32)
    other = other.astype(f32)
    pat0 = jnp.where(is_first, own, other)
    pat1 = jnp.where(is_first, other, own)

    def rows_of(pat):
        return jnp.concatenate([pat[:, 0:6], pat[:, 6:12]], axis=0)

    def member(pat):
        iota = lax.broadcasted_iota(jnp.int32, (64, 64), 1).astype(f32)
        total = jnp.zeros((64, 64), f32)
        for s in range(6):
            total = total + jnp.where(pat[:, s:s + 1] == iota, 1.0, 0.0)
        return total

    def mask(cond):
        return jnp.where(cond, 1.0, 0.0)

    p0, p1 = rows_of(pat0), rows_of(pat1)
    m0, m1 = member(p0), member(p1)
    m0b, m1b = m0.astype(bf16), m1.astype(bf16)
    common = dot_nt(m0b, m0b)
    reach2 = mask(common > 1.0)
    b2 = reach2.astype(bf16)
    reach4 = mask(dot_nn(b2, b2) > 0.5)
    b4 = reach4.astype(bf16)
    b8 = mask(dot_nn(b4, b4) > 0.5).astype(bf16)
    lane = lax.broadcasted_iota(jnp.int32, (1, 64), 1).astype(f32)
    sub = lax.broadcasted_iota(jnp.int32, (64, 64), 0).astype(f32)
    first = common[0:1, :]
    start = jnp.min(jnp.where(first == 4.0, lane, 1000.0), axis=1, keepdims=True)
    second = jnp.sum(jnp.where(sub == start, common, 0.0), axis=0, keepdims=True)
    t = jnp.concatenate([mask(first > 5.0), mask(first > 3.0), mask(second > 5.0), mask(second > 3.0)], axis=0)
    for b in (b2, b4, b8):
        t = jnp.concatenate([t, mask(dot_nn(t.astype(bf16), b) > 0.5)], axis=0)
    which = lax.broadcasted_iota(jnp.int32, (32, 64), 0)
    from_first = jnp.bitwise_and(which, 3) < 2
    dist0 = 16.0 - jnp.sum(jnp.where(from_first, t, 0.0), axis=0, keepdims=True)
    dist1 = 16.0 - jnp.sum(jnp.where(from_first, 0.0, t), axis=0, keepdims=True)
    pos0 = jnp.where(dist1 < dist0, dist0, jnp.where(dist0 == 0.0, 0.0, 32.0 - dist0))
    group = lax.broadcasted_iota(jnp.int32, (32, 64), 0).astype(f32)
    g0 = mask(group == pos0)

    def centre(c):
        return mask(roll_groups(c, -1) + c + roll_groups(c, 1) > 5.0)

    hc = centre(dot_nn(g0.astype(bf16), m0b))
    g1 = centre(dot_nt(hc.astype(bf16), m1b))
    gr = jnp.where(is_first, g0, g1)
    pr = jnp.where(is_first, p0, p1)

    lanes = lax.broadcasted_iota(jnp.int32, (32, 64), 1)
    natural = (jnp.bitwise_and(lanes, 31) * 2 + jnp.right_shift(lanes, 5)).astype(f32)
    column = lanes.astype(f32)
    row_lo = jnp.min(jnp.where(gr > 0.5, natural, 1000.0), axis=1, keepdims=True)
    row_hi = jnp.max(jnp.where(gr > 0.5, natural, -1.0), axis=1, keepdims=True)
    col_lo = jnp.min(jnp.where(hc > 0.5, column, 1000.0), axis=1, keepdims=True)
    col_hi = jnp.max(jnp.where(hc > 0.5, column, -1.0), axis=1, keepdims=True)

    prb = jnp.concatenate([pr, jnp.zeros((64, 122), f32)], axis=1).astype(bf16)
    out_lane = lax.broadcasted_iota(jnp.int32, (32, 128), 1)
    slot_iota = out_lane.astype(f32)
    table = jnp.zeros((32, 128), f32)
    for a, members in enumerate((row_lo, row_hi)):
        chosen = mask((gr > 0.5) & (natural == members))
        cols = dot_nn(chosen.astype(bf16), prb)
        cols = jnp.where(out_lane < 6, cols, -1.0)
        for d in range(3):
            for j, cmem in enumerate((col_lo, col_hi)):
                target = roll_groups(cmem, d - 1) if d != 1 else cmem
                slot = jnp.sum(jnp.where(cols == target, slot_iota, 0.0), axis=1, keepdims=True)
                table = jnp.where(out_lane == a * 6 + d * 2 + j, members * 6.0 + slot, table)
    tin = jnp.clip(table, 0.0, 383.0).astype(jnp.int32)

    eye = mask(lax.broadcasted_iota(jnp.int32, (64, 64), 0) == lax.broadcasted_iota(jnp.int32, (64, 64), 1)).astype(bf16)
    extra = lax.broadcasted_iota(jnp.int32, (32, 64), 0).astype(f32)
    grt = dot_nt(eye, gr.astype(bf16))
    gi = jnp.sum(grt * lax.broadcasted_iota(jnp.int32, (64, 32), 1).astype(f32), axis=1, keepdims=True)
    hi_flag = mask((gr > 0.5) & (natural == row_hi))
    ai = jnp.sum(dot_nt(eye, hi_flag.astype(bf16)), axis=1, keepdims=True)
    gcol = jnp.sum(hc * extra, axis=0, keepdims=True)
    jcol = jnp.sum(mask((hc > 0.5) & (column == col_hi)), axis=0, keepdims=True)
    code = gcol * 2.0 + jcol
    iota64 = lax.broadcasted_iota(jnp.int32, (64, 64), 1).astype(f32)
    lane64 = lax.broadcasted_iota(jnp.int32, (64, 128), 1)
    out = jnp.zeros((64, 128), jnp.int32)
    gi_i, ai_i = gi.astype(jnp.int32), ai.astype(jnp.int32)
    for s in range(6):
        val = jnp.sum(jnp.where(pr[:, s:s + 1] == iota64, code, 0.0), axis=1, keepdims=True).astype(jnp.int32)
        gc, jc = jnp.right_shift(val, 1), jnp.bitwise_and(val, 1)
        d = jnp.bitwise_and(gi_i - gc + 1, 31)
        out = jnp.where(lane64 == s, gc * 12 + jc * 6 + d * 2 + ai_i, out)
    return tin, jnp.clip(out, 0, 383)


def inside(place):
    return jnp.minimum(jnp.maximum(place, 0), NL * 12 - 1)


def split(value):
    high = value.astype(jnp.bfloat16)
    return high, (value - high.astype(jnp.float32)).astype(jnp.bfloat16)


def multiply(row, col, xs, hi, lo, y, wait_other, send_half):
    def put(part, r, a, c, j, block):
        rows = pl.ds(pl.multiple_of(r * 256 + a * 128, 128), 128)
        cols = pl.ds(pl.multiple_of(c * 256 + j * 128, 128), 128)
        high, low = split(block)
        hi[part, rows, cols] = high
        lo[part, rows, cols] = low

    def piece(r, n):
        return xs[r, n].reshape(BLK, BLK)

    def assemble(r):
        @pl.loop(0, 8)
        def _(n):
            c, a, j = n // 4, lax.rem(n // 2, 2), lax.rem(n, 2)
            base = MAIN * lax.rem(r + c, 2) + a * 2 + j
            put(3, r, a, c, j, piece(r, base))
            put(4, r, a, c, j, piece(r, base + 4))

        @pl.loop(0, 3)
        def _(part):
            put(part, r, 0, r, 0, piece(r, 8 + part * 2))
            mixed = piece(r, 9 + part * 2)
            put(part, r, 0, r, 1, mixed)
            put(part, r, 1, r, 0, mixed.T)
            put(part, r, 1, r, 1, piece(r, 14 + part))
            for e, (at, aj) in enumerate(((0, r), (r, 1))):
                block = piece(r, MAIN + 8 + part * 2 + e)
                put(part, r, at, 1 - r, aj, block)
                put(part, 1 - r, aj, r, at, block.T)

    assemble(row)
    wait_other()
    assemble(1 - row)

    def mul(pairs, half=None):
        total = None
        for (stacked, high), part, transposed in pairs:
            if half is None:
                bh, bl = hi[part], lo[part]
            elif transposed:
                bh, bl = hi[part, half, :], lo[part, half, :]
            else:
                bh, bl = hi[part, :, half], lo[part, :, half]
            dot = dot_nt if transposed else dot_nn
            both = dot(stacked, bh)
            term = both[:BLK] + both[BLK:] + dot(high, bl)
            total = term if total is None else total + term
        return total

    def apply(w, half=None):
        left, mid, right = w
        return (
            mul([(left, 0, False), (mid, 3, False)], half),
            mul([(left, 3, True), (mid, 1, False), (right, 4, True)], half),
            mul([(mid, 4, False), (right, 2, False)], half),
        )

    def stack(high, low):
        return jnp.concatenate([high, low], axis=0), high

    offset = col * 256 + row * 128
    mine = pl.ds(pl.multiple_of(offset, 128), 128)
    left, mid, right = apply([stack(hi[part, mine, :], lo[part, mine, :]) for part in (3, 1, 4)])
    q = lax.broadcasted_iota(jnp.int32, (BLK, 512), 0)
    k = lax.broadcasted_iota(jnp.int32, (BLK, 512), 1)
    mid = jnp.where(k == q + offset, 3.0, 0.0) - mid
    s = [stack(*split(-left)), stack(*split(mid)), stack(*split(-right))]
    for r in range(2):
        for d, part in enumerate(apply(s, slice(r * 256, r * 256 + 256))):
            half = 0.5 * part
            for a in range(2):
                y[r, d * 2 + a] = half[:, a * 128:a * 128 + 128].T.reshape(NL, ROWS, BLK)
        send_half(r)


def kernel(
    cols_ref, x_ref, out_ref, pat, own, other, tin_v, tout_v, tin, tout, buf, stage, xs, hi, lo, y, srt, stage2,
    psend, precv, send1, recv1, send2, recv2, swap_send, swap_recv, send3, recv3, send4, recv4, core, local,
):
    me, row, col = my_ids()
    barrier = pltpu.get_barrier_semaphore()

    def signal(device):
        pl.semaphore_signal(barrier, inc=1, device_id=device, device_id_type=MESH)

    signal((me, 1 - row, col))
    signal((me, row, 1 - col))

    @pl.loop(1, NL)
    def _(k):
        signal((lax.rem(me + k, NL), row, col))

    for jj in range(2):
        pat[0:1, jj * 6:jj * 6 + 6] = cols_ref[0, jj]
    pl.semaphore_wait(barrier, NL + 1)

    def remote(src, dst, send, recv, device):
        return pltpu.make_async_remote_copy(src, dst, send, recv, device_id=device, device_id_type=MESH)

    def others(step):
        @pl.loop(1, NL)
        def _(k):
            step(lax.rem(me + k, NL))

    def start_others(step):
        @pl.loop(0, NL)
        def _(k):
            p = lax.rem((STRIDE + 4 * row) * k + me, NL)
            pl.when(p != me)(lambda: step(p))

    def wait_bytes(ref, sem):
        pltpu.make_async_copy(ref, ref, sem).wait()

    def pattern_copy(p):
        return remote(pat, own.at[me], psend, precv, (p, row, col))

    def spread(p):
        return remote(x_ref.at[:, p], buf.at[pl.ds(me * 12, 12)], send1, recv1, (p, row, col))

    start_others(lambda p: pattern_copy(p).start())
    start_others(lambda p: spread(p).start())
    here1 = pltpu.make_async_copy(x_ref.at[:, me], buf.at[pl.ds(me * 12, 12)], local.at[0])
    here1.start()
    own[me] = pat[...]
    wait_bytes(own.at[pl.ds(0, NL - 1)], precv)
    swap_pattern = remote(own, other, core.at[0], core.at[1], (me, 1 - row, col))
    swap_pattern.start()
    swap_pattern.wait()
    tin_v[...], tout_v[...] = order_tables(row, own[...].reshape(NL, 128), other[...].reshape(NL, 128))
    moves = [
        pltpu.make_async_copy(vector, scalar, local.at[1 + n])
        for n, (vector, scalar) in enumerate(((tin_v, tin), (tout_v, tout)))
    ]
    for move in moves:
        move.start()
    for move in moves:
        move.wait()
    here1.wait()
    wait_bytes(buf.at[pl.ds(0, (NL - 1) * 12)], recv1)

    def deliver(h, c, source, same):
        base, count = (0, MAIN) if same else (MAIN, SIDE)
        return remote(
            stage.at[h, pl.ds(0, count)], xs.at[row, pl.ds(base, count), source],
            send2.at[c, h], recv2.at[1 - int(same), source], (h, row, c))

    lower = row * (1 - col)

    def fill(h):
        for a in range(2):
            for j in range(2):
                stage[h, a * 2 + j] = buf[inside(tin[h, a * 6 + j])]
                stage[h, 4 + a * 2 + j] = buf[inside(tin[h, a * 6 + 4 + j])]
        for n, g in enumerate((lax.rem(h + NL - 1, NL), h, lax.rem(h + 1, NL))):
            stage[h, 8 + n * 2] = buf[inside(tin[g, 2 + lower])]
            stage[h, 9 + n * 2] = buf[inside(tin[g, 3 + 6 * lower])]
            stage[h, 14 + n] = buf[inside(tin[g, 9])]

    def by_class(step):
        for same in (True, False):
            pl.when((row == col) if same else (row != col))(functools.partial(step, same))

    def send_pieces(same):
        def step(h):
            fill(h)
            deliver(h, col, me, same).start()
            deliver(h, 1 - col, me, same).start()

        start_others(step)
        fill(me)
        deliver(me, 1 - col, me, same).start()
        base, count = (0, MAIN) if same else (MAIN, SIDE)
        here = pltpu.make_async_copy(stage.at[me, pl.ds(0, count)], xs.at[row, pl.ds(base, count), me], local.at[3])
        here.start()
        here.wait()

    by_class(send_pieces)
    wait_bytes(own.at[pl.ds(0, NL - 1)], psend)
    wait_bytes(buf.at[pl.ds(0, (NL - 1) * 12)], send1)

    def swap(p, r):
        return remote(xs.at[r, :, p], xs.at[r, :, p], swap_send, swap_recv, (me, 1 - row, col))

    @pl.loop(1, NL)
    def _(k):
        p = lax.rem(me + NL - k, NL)
        deliver(me, col, p, True).wait_recv()
        deliver(me, col, p, False).wait_recv()
        swap(p, row).start()

    by_class(lambda same: deliver(me, col, me, not same).wait_recv())
    swap(me, row).start()

    def result(p, r):
        return remote(y.at[r, :, p], srt.at[pl.ds(me * 12 + row * 6, 6)], send3, recv3, (p, r, col))

    here3 = pltpu.make_async_copy(y.at[row, :, me], srt.at[pl.ds(me * 12 + row * 6, 6)], local.at[4])

    def send_half(r):
        start_others(lambda p: result(p, r).start())

        @pl.when(r == row)
        def _():
            here3.start()

        @pl.when(r != row)
        def _():
            result(me, r).start()

    multiply(row, col, xs, hi, lo, y, lambda: wait_bytes(xs.at[1 - row], swap_recv), send_half)

    def sent_pieces(same):
        others(lambda p: deliver(p, col, me, same).wait_send())
        others(lambda p: deliver(p, 1 - col, me, same).wait_send())
        deliver(me, 1 - col, me, same).wait_send()

    by_class(sent_pieces)
    wait_bytes(xs.at[row], swap_send)
    here3.wait()
    wait_bytes(srt.at[pl.ds(0, (2 * NL - 1) * 6)], recv3)

    def home(p):
        return remote(stage2.at[p], out_ref.at[:, me], send4, recv4, (p, row, col))

    def fill_home(p):
        for jj in range(2):
            for s in range(6):
                stage2[p, jj * 6 + s] = srt[inside(tout[jj * 32 + p, s])]

    def go_home(p):
        fill_home(p)
        home(p).start()

    start_others(go_home)
    fill_home(me)
    here4 = pltpu.make_async_copy(stage2.at[me], out_ref.at[:, me], local.at[5])
    here4.start()
    wait_bytes(srt.at[pl.ds(0, (2 * NL - 1) * 6)], send3)
    wait_bytes(stage2.at[pl.ds(0, NL - 1)], send4)
    here4.wait()
    wait_bytes(stage2.at[pl.ds(0, NL - 1)], recv4)


ANY = pl.BlockSpec(memory_space=pl.ANY)
VMEM = pl.BlockSpec(memory_space=pltpu.VMEM)


def body(x_blocks, block_cols):
    f32, bf16, i32 = jnp.float32, jnp.bfloat16, jnp.int32
    vmem, smem, dma = pltpu.VMEM, pltpu.SMEM, pltpu.SemaphoreType.DMA
    out = pl.pallas_call(
        kernel,
        out_shape=jax.ShapeDtypeStruct((12, NL, ROWS, BLK), f32),
        in_specs=[VMEM, ANY],
        out_specs=ANY,
        scratch_shapes=[
            vmem((1, 128), i32), vmem((NL, 1, 128), i32), vmem((NL, 1, 128), i32),
            vmem((32, 128), i32), vmem((64, 128), i32), smem((32, 128), i32), smem((64, 128), i32),
            vmem((NL * 12, ROWS, BLK), f32), vmem((NL, MAIN, ROWS, BLK), f32), vmem((2, MAIN + SIDE, NL, ROWS, BLK), f32),
            vmem((5, 512, 512), bf16), vmem((5, 512, 512), bf16),
            vmem((2, 6, NL, ROWS, BLK), f32), vmem((NL * 12, ROWS, BLK), f32), vmem((NL, 12, ROWS, BLK), f32),
            dma, dma, dma, dma, dma((2, NL)), dma((2, NL)), dma, dma,
            dma, dma, dma, dma, dma((2,)), dma((6,)),
        ],
        compiler_params=pltpu.CompilerParams(
            collective_id=0, has_side_effects=True, vmem_limit_bytes=VMEM_LIMIT),
        name="step",
    )(block_cols, x_blocks.reshape(12, NL, ROWS, BLK))
    return out.reshape(x_blocks.shape)


def solution(mesh):
    return jax.shard_map(
        body,
        mesh=mesh,
        in_specs=(P("row", "layer", "col", None, None, None), P("row", "layer", "col", None)),
        out_specs=P("row", "layer", "col", None, None, None),
        check_vma=False,
    )
```

```python
import functools

import jax
import jax.numpy as jnp
from jax import lax
from jax.experimental import pallas as pl
from jax.experimental.pallas import tpu as pltpu
from jax.sharding import PartitionSpec as P

MESH = pl.DeviceIdType.MESH
NL = 32
ROWS = 4
BLK = 128
MAIN = 17
SIDE = 14
STRIDE = 3
VMEM_LIMIT = 56 * 1024 * 1024


def my_ids():
    return lax.axis_index("layer"), lax.axis_index("row"), lax.axis_index("col")


def dot_nt(a, b):
    return lax.dot_general(a, b, (((1,), (1,)), ((), ())), preferred_element_type=jnp.float32)


def dot_nn(a, b):
    return jnp.dot(a, b, preferred_element_type=jnp.float32)


def roll_groups(a, shift):
    return jnp.concatenate([a[shift:], a[:shift]], axis=0)


def order_tables(row, own, other):
    f32, bf16 = jnp.float32, jnp.bfloat16
    is_first = row == 0
    own = own.astype(f32)
    other = other.astype(f32)
    pat0 = jnp.where(is_first, own, other)
    pat1 = jnp.where(is_first, other, own)

    def rows_of(pat):
        return jnp.concatenate([pat[:, 0:6], pat[:, 6:12]], axis=0)

    def member(pat):
        iota = lax.broadcasted_iota(jnp.int32, (64, 64), 1).astype(f32)
        total = jnp.zeros((64, 64), f32)
        for s in range(6):
            total = total + jnp.where(pat[:, s:s + 1] == iota, 1.0, 0.0)
        return total

    def mask(cond):
        return jnp.where(cond, 1.0, 0.0)

    p0, p1 = rows_of(pat0), rows_of(pat1)
    m0, m1 = member(p0), member(p1)
    m0b, m1b = m0.astype(bf16), m1.astype(bf16)
    common = dot_nt(m0b, m0b)
    reach2 = mask(common > 1.0)
    b2 = reach2.astype(bf16)
    reach4 = mask(dot_nn(b2, b2) > 0.5)
    b4 = reach4.astype(bf16)
    b8 = mask(dot_nn(b4, b4) > 0.5).astype(bf16)
    lane = lax.broadcasted_iota(jnp.int32, (1, 64), 1).astype(f32)
    sub = lax.broadcasted_iota(jnp.int32, (64, 64), 0).astype(f32)
    first = common[0:1, :]
    start = jnp.min(jnp.where(first == 4.0, lane, 1000.0), axis=1, keepdims=True)
    second = jnp.sum(jnp.where(sub == start, common, 0.0), axis=0, keepdims=True)
    t = jnp.concatenate([mask(first > 5.0), mask(first > 3.0), mask(second > 5.0), mask(second > 3.0)], axis=0)
    for b in (b2, b4, b8):
        t = jnp.concatenate([t, mask(dot_nn(t.astype(bf16), b) > 0.5)], axis=0)
    which = lax.broadcasted_iota(jnp.int32, (32, 64), 0)
    from_first = jnp.bitwise_and(which, 3) < 2
    dist0 = 16.0 - jnp.sum(jnp.where(from_first, t, 0.0), axis=0, keepdims=True)
    dist1 = 16.0 - jnp.sum(jnp.where(from_first, 0.0, t), axis=0, keepdims=True)
    pos0 = jnp.where(dist1 < dist0, dist0, jnp.where(dist0 == 0.0, 0.0, 32.0 - dist0))
    group = lax.broadcasted_iota(jnp.int32, (32, 64), 0).astype(f32)
    g0 = mask(group == pos0)

    def centre(c):
        return mask(roll_groups(c, -1) + c + roll_groups(c, 1) > 5.0)

    hc = centre(dot_nn(g0.astype(bf16), m0b))
    g1 = centre(dot_nt(hc.astype(bf16), m1b))
    gr = jnp.where(is_first, g0, g1)
    pr = jnp.where(is_first, p0, p1)

    lanes = lax.broadcasted_iota(jnp.int32, (32, 64), 1)
    natural = (jnp.bitwise_and(lanes, 31) * 2 + jnp.right_shift(lanes, 5)).astype(f32)
    column = lanes.astype(f32)
    row_lo = jnp.min(jnp.where(gr > 0.5, natural, 1000.0), axis=1, keepdims=True)
    row_hi = jnp.max(jnp.where(gr > 0.5, natural, -1.0), axis=1, keepdims=True)
    col_lo = jnp.min(jnp.where(hc > 0.5, column, 1000.0), axis=1, keepdims=True)
    col_hi = jnp.max(jnp.where(hc > 0.5, column, -1.0), axis=1, keepdims=True)

    prb = jnp.concatenate([pr, jnp.zeros((64, 122), f32)], axis=1).astype(bf16)
    out_lane = lax.broadcasted_iota(jnp.int32, (32, 128), 1)
    slot_iota = out_lane.astype(f32)
    table = jnp.zeros((32, 128), f32)
    for a, members in enumerate((row_lo, row_hi)):
        chosen = mask((gr > 0.5) & (natural == members))
        cols = dot_nn(chosen.astype(bf16), prb)
        cols = jnp.where(out_lane < 6, cols, -1.0)
        for d in range(3):
            for j, cmem in enumerate((col_lo, col_hi)):
                target = roll_groups(cmem, d - 1) if d != 1 else cmem
                slot = jnp.sum(jnp.where(cols == target, slot_iota, 0.0), axis=1, keepdims=True)
                table = jnp.where(out_lane == a * 6 + d * 2 + j, members * 6.0 + slot, table)
    tin = jnp.clip(table, 0.0, 383.0).astype(jnp.int32)

    eye = mask(lax.broadcasted_iota(jnp.int32, (64, 64), 0) == lax.broadcasted_iota(jnp.int32, (64, 64), 1)).astype(bf16)
    extra = lax.broadcasted_iota(jnp.int32, (32, 64), 0).astype(f32)
    grt = dot_nt(eye, gr.astype(bf16))
    gi = jnp.sum(grt * lax.broadcasted_iota(jnp.int32, (64, 32), 1).astype(f32), axis=1, keepdims=True)
    hi_flag = mask((gr > 0.5) & (natural == row_hi))
    ai = jnp.sum(dot_nt(eye, hi_flag.astype(bf16)), axis=1, keepdims=True)
    gcol = jnp.sum(hc * extra, axis=0, keepdims=True)
    jcol = jnp.sum(mask((hc > 0.5) & (column == col_hi)), axis=0, keepdims=True)
    code = gcol * 2.0 + jcol
    iota64 = lax.broadcasted_iota(jnp.int32, (64, 64), 1).astype(f32)
    lane64 = lax.broadcasted_iota(jnp.int32, (64, 128), 1)
    out = jnp.zeros((64, 128), jnp.int32)
    gi_i, ai_i = gi.astype(jnp.int32), ai.astype(jnp.int32)
    for s in range(6):
        val = jnp.sum(jnp.where(pr[:, s:s + 1] == iota64, code, 0.0), axis=1, keepdims=True).astype(jnp.int32)
        gc, jc = jnp.right_shift(val, 1), jnp.bitwise_and(val, 1)
        d = jnp.bitwise_and(gi_i - gc + 1, 31)
        out = jnp.where(lane64 == s, gc * 12 + jc * 6 + d * 2 + ai_i, out)
    return tin, jnp.clip(out, 0, 383)


def inside(place):
    return jnp.minimum(jnp.maximum(place, 0), NL * 12 - 1)


def split(value):
    high = value.astype(jnp.bfloat16)
    return high, (value - high.astype(jnp.float32)).astype(jnp.bfloat16)


def multiply(row, col, xs, hi, lo, y, wait_other, send_half):
    def put(part, r, a, c, j, block):
        rows = pl.ds(pl.multiple_of(r * 256 + a * 128, 128), 128)
        cols = pl.ds(pl.multiple_of(c * 256 + j * 128, 128), 128)
        high, low = split(block)
        hi[part, rows, cols] = high
        lo[part, rows, cols] = low

    def piece(r, n):
        return xs[r, n].reshape(BLK, BLK)

    def assemble(r):
        @pl.loop(0, 8)
        def _(n):
            c, a, j = n // 4, lax.rem(n // 2, 2), lax.rem(n, 2)
            base = MAIN * lax.rem(r + c, 2) + a * 2 + j
            put(3, r, a, c, j, piece(r, base))
            put(4, r, a, c, j, piece(r, base + 4))

        @pl.loop(0, 3)
        def _(part):
            put(part, r, 0, r, 0, piece(r, 8 + part * 2))
            mixed = piece(r, 9 + part * 2)
            put(part, r, 0, r, 1, mixed)
            put(part, r, 1, r, 0, mixed.T)
            put(part, r, 1, r, 1, piece(r, 14 + part))
            for e, (at, aj) in enumerate(((0, r), (r, 1))):
                block = piece(r, MAIN + 8 + part * 2 + e)
                put(part, r, at, 1 - r, aj, block)
                put(part, 1 - r, aj, r, at, block.T)

    assemble(row)
    wait_other()
    assemble(1 - row)

    def mul(pairs, half=None):
        total = None
        for (stacked, high), part, transposed in pairs:
            if half is None:
                bh, bl = hi[part], lo[part]
            elif transposed:
                bh, bl = hi[part, half, :], lo[part, half, :]
            else:
                bh, bl = hi[part, :, half], lo[part, :, half]
            dot = dot_nt if transposed else dot_nn
            both = dot(stacked, bh)
            term = both[:BLK] + both[BLK:] + dot(high, bl)
            total = term if total is None else total + term
        return total

    def apply(w, half=None):
        left, mid, right = w
        return (
            mul([(left, 0, False), (mid, 3, False)], half),
            mul([(left, 3, True), (mid, 1, False), (right, 4, True)], half),
            mul([(mid, 4, False), (right, 2, False)], half),
        )

    def stack(high, low):
        return jnp.concatenate([high, low], axis=0), high

    offset = col * 256 + row * 128
    mine = pl.ds(pl.multiple_of(offset, 128), 128)
    left, mid, right = apply([stack(hi[part, mine, :], lo[part, mine, :]) for part in (3, 1, 4)])
    q = lax.broadcasted_iota(jnp.int32, (BLK, 512), 0)
    k = lax.broadcasted_iota(jnp.int32, (BLK, 512), 1)
    mid = jnp.where(k == q + offset, 3.0, 0.0) - mid
    s = [stack(*split(-left)), stack(*split(mid)), stack(*split(-right))]
    for r in range(2):
        for d, part in enumerate(apply(s, slice(r * 256, r * 256 + 256))):
            half = 0.5 * part
            for a in range(2):
                y[r, d * 2 + a] = half[:, a * 128:a * 128 + 128].T.reshape(NL, ROWS, BLK)
        send_half(r)


def kernel(
    cols_ref, x_ref, out_ref, pat, own, other, tin_v, tout_v, tin, tout, buf, stage, xs, hi, lo, y, srt, stage2,
    psend, precv, send1, recv1, send2, recv2, swap_send, swap_recv, send3, recv3, send4, recv4, core, local,
):
    me, row, col = my_ids()
    barrier = pltpu.get_barrier_semaphore()

    def signal(device):
        pl.semaphore_signal(barrier, inc=1, device_id=device, device_id_type=MESH)

    signal((me, 1 - row, col))
    signal((me, row, 1 - col))

    @pl.loop(1, NL)
    def _(k):
        signal((lax.rem(me + k, NL), row, col))

    for jj in range(2):
        pat[0:1, jj * 6:jj * 6 + 6] = cols_ref[0, jj]
    pl.semaphore_wait(barrier, NL + 1)

    def remote(src, dst, send, recv, device):
        return pltpu.make_async_remote_copy(src, dst, send, recv, device_id=device, device_id_type=MESH)

    def others(step):
        @pl.loop(1, NL)
        def _(k):
            step(lax.rem(me + k, NL))

    def start_others(step):
        @pl.loop(0, NL)
        def _(k):
            p = lax.rem((STRIDE + 4 * row) * k + me, NL)
            pl.when(p != me)(lambda: step(p))

    def wait_bytes(ref, sem):
        pltpu.make_async_copy(ref, ref, sem).wait()

    def pattern_copy(p):
        return remote(pat, own.at[me], psend, precv, (p, row, col))

    def spread(p):
        return remote(x_ref.at[:, p], buf.at[pl.ds(me * 12, 12)], send1, recv1, (p, row, col))

    start_others(lambda p: pattern_copy(p).start())
    start_others(lambda p: spread(p).start())
    here1 = pltpu.make_async_copy(x_ref.at[:, me], buf.at[pl.ds(me * 12, 12)], local.at[0])
    here1.start()
    own[me] = pat[...]
    wait_bytes(own.at[pl.ds(0, NL - 1)], precv)
    swap_pattern = remote(own, other, core.at[0], core.at[1], (me, 1 - row, col))
    swap_pattern.start()
    swap_pattern.wait()
    tin_v[...], tout_v[...] = order_tables(row, own[...].reshape(NL, 128), other[...].reshape(NL, 128))
    moves = [
        pltpu.make_async_copy(vector, scalar, local.at[1 + n])
        for n, (vector, scalar) in enumerate(((tin_v, tin), (tout_v, tout)))
    ]
    for move in moves:
        move.start()
    for move in moves:
        move.wait()
    here1.wait()
    wait_bytes(buf.at[pl.ds(0, (NL - 1) * 12)], recv1)

    def deliver(h, c, source, same):
        base, count = (0, MAIN) if same else (MAIN, SIDE)
        return remote(
            stage.at[h, pl.ds(0, count)], xs.at[row, pl.ds(base, count), source],
            send2.at[c, h], recv2.at[1 - int(same), source], (h, row, c))

    lower = row * (1 - col)

    def fill(h):
        for a in range(2):
            for j in range(2):
                stage[h, a * 2 + j] = buf[inside(tin[h, a * 6 + j])]
                stage[h, 4 + a * 2 + j] = buf[inside(tin[h, a * 6 + 4 + j])]
        for n, g in enumerate((lax.rem(h + NL - 1, NL), h, lax.rem(h + 1, NL))):
            stage[h, 8 + n * 2] = buf[inside(tin[g, 2 + lower])]
            stage[h, 9 + n * 2] = buf[inside(tin[g, 3 + 6 * lower])]
            stage[h, 14 + n] = buf[inside(tin[g, 9])]

    def by_class(step):
        for same in (True, False):
            pl.when((row == col) if same else (row != col))(functools.partial(step, same))

    def send_pieces(same):
        def step(h):
            fill(h)
            nearer = lax.rem(col + row, 2)
            deliver(h, nearer, me, same).start()
            deliver(h, 1 - nearer, me, same).start()

        start_others(step)
        fill(me)
        deliver(me, 1 - col, me, same).start()
        base, count = (0, MAIN) if same else (MAIN, SIDE)
        here = pltpu.make_async_copy(stage.at[me, pl.ds(0, count)], xs.at[row, pl.ds(base, count), me], local.at[3])
        here.start()
        here.wait()

    by_class(send_pieces)
    wait_bytes(own.at[pl.ds(0, NL - 1)], psend)
    wait_bytes(buf.at[pl.ds(0, (NL - 1) * 12)], send1)

    def swap(p, r):
        return remote(xs.at[r, :, p], xs.at[r, :, p], swap_send, swap_recv, (me, 1 - row, col))

    @pl.loop(1, NL)
    def _(k):
        p = lax.rem(me + NL - k, NL)
        deliver(me, col, p, True).wait_recv()
        deliver(me, col, p, False).wait_recv()
        swap(p, row).start()

    by_class(lambda same: deliver(me, col, me, not same).wait_recv())
    swap(me, row).start()

    def result(p, r):
        return remote(y.at[r, :, p], srt.at[pl.ds(me * 12 + row * 6, 6)], send3, recv3, (p, r, col))

    here3 = pltpu.make_async_copy(y.at[row, :, me], srt.at[pl.ds(me * 12 + row * 6, 6)], local.at[4])

    def send_half(r):
        start_others(lambda p: result(p, r).start())

        @pl.when(r == row)
        def _():
            here3.start()

        @pl.when(r != row)
        def _():
            result(me, r).start()

    multiply(row, col, xs, hi, lo, y, lambda: wait_bytes(xs.at[1 - row], swap_recv), send_half)

    def sent_pieces(same):
        others(lambda p: deliver(p, col, me, same).wait_send())
        others(lambda p: deliver(p, 1 - col, me, same).wait_send())
        deliver(me, 1 - col, me, same).wait_send()

    by_class(sent_pieces)
    wait_bytes(xs.at[row], swap_send)
    here3.wait()
    wait_bytes(srt.at[pl.ds(0, (2 * NL - 1) * 6)], recv3)

    def home(p):
        return remote(stage2.at[p], out_ref.at[:, me], send4, recv4, (p, row, col))

    def fill_home(p):
        for jj in range(2):
            for s in range(6):
                stage2[p, jj * 6 + s] = srt[inside(tout[jj * 32 + p, s])]

    def go_home(p):
        fill_home(p)
        home(p).start()

    start_others(go_home)
    fill_home(me)
    here4 = pltpu.make_async_copy(stage2.at[me], out_ref.at[:, me], local.at[5])
    here4.start()
    wait_bytes(srt.at[pl.ds(0, (2 * NL - 1) * 6)], send3)
    wait_bytes(stage2.at[pl.ds(0, NL - 1)], send4)
    here4.wait()
    wait_bytes(stage2.at[pl.ds(0, NL - 1)], recv4)


ANY = pl.BlockSpec(memory_space=pl.ANY)
VMEM = pl.BlockSpec(memory_space=pltpu.VMEM)


def finish(in_ref, out_ref, vm, sems, sems2):
    first = [pltpu.make_async_copy(in_ref.at[pl.ds(2 * n, 2)], vm.at[pl.ds(2 * n, 2)], sems.at[n]) for n in range(6)]
    second = [pltpu.make_async_copy(vm.at[pl.ds(2 * n, 2)], out_ref.at[pl.ds(2 * n, 2)], sems2.at[n]) for n in range(6)]
    for part in first:
        part.start()
    for part, after in zip(first, second):
        part.wait()
        after.start()
    for part in second:
        part.wait()


def body(x_blocks, block_cols):
    f32, bf16, i32 = jnp.float32, jnp.bfloat16, jnp.int32
    vmem, smem, dma = pltpu.VMEM, pltpu.SMEM, pltpu.SemaphoreType.DMA
    out = pl.pallas_call(
        kernel,
        out_shape=jax.ShapeDtypeStruct((12, NL, ROWS, BLK), f32),
        in_specs=[VMEM, ANY],
        out_specs=ANY,
        scratch_shapes=[
            vmem((1, 128), i32), vmem((NL, 1, 128), i32), vmem((NL, 1, 128), i32),
            vmem((32, 128), i32), vmem((64, 128), i32), smem((32, 128), i32), smem((64, 128), i32),
            vmem((NL * 12, ROWS, BLK), f32), vmem((NL, MAIN, ROWS, BLK), f32), vmem((2, MAIN + SIDE, NL, ROWS, BLK), f32),
            vmem((5, 512, 512), bf16), vmem((5, 512, 512), bf16),
            vmem((2, 6, NL, ROWS, BLK), f32), vmem((NL * 12, ROWS, BLK), f32), vmem((NL, 12, ROWS, BLK), f32),
            dma, dma, dma, dma, dma((2, NL)), dma((2, NL)), dma, dma,
            dma, dma, dma, dma, dma((2,)), dma((6,)),
        ],
        compiler_params=pltpu.CompilerParams(
            collective_id=0, has_side_effects=True, vmem_limit_bytes=VMEM_LIMIT),
        name="step",
    )(block_cols, x_blocks.reshape(12, NL, ROWS, BLK))
    out = pl.pallas_call(
        finish,
        out_shape=jax.ShapeDtypeStruct((12, BLK, BLK), f32),
        in_specs=[ANY],
        out_specs=ANY,
        scratch_shapes=[vmem((12, BLK, BLK), f32), dma((6,)), dma((6,))],
        name="finish",
    )(out.reshape(12, BLK, BLK))
    return out.reshape(x_blocks.shape)


def solution(mesh):
    return jax.shard_map(
        body,
        mesh=mesh,
        in_specs=(P("row", "layer", "col", None, None, None), P("row", "layer", "col", None)),
        out_specs=P("row", "layer", "col", None, None, None),
        check_vma=False,
    )
```
